32 devices in a mesh: grp: 2 (over x), smp: 16 (over z, y, core).
Axes of the slice: x: 2, y: 2, z: 4, core: 2. Of those that a mesh axis runs over, the one named last changes fastest.
Arguments:
- activations: bfloat16 [64, 384, 768], P(('grp', 'smp')), parts along dimension 0, may hold values from -24 to 24
- cotangent: bfloat16 [64, 384, 768], P(('grp', 'smp')), parts along dimension 0, may hold values from -6 to 6
- pair_rep: bfloat16 [768, 384, 128], P(('grp', 'smp')), parts along dimension 0, may hold values from -6 to 6
- pair_gain: float32 [128], replicated, may hold values from 0.5 to 1.5
- w_pair: bfloat16 [128, 16], replicated, may hold values from -0.5 to 0.5
- w_query: bfloat16 [768, 768], replicated, may hold values from -0.21875 to 0.21875
- w_key: bfloat16 [768, 768], replicated, may hold values from -0.21875 to 0.21875
- w_value: bfloat16 [768, 768], replicated, may hold values from -0.21875 to 0.21875
- w_out: bfloat16 [768, 768], replicated, may hold values from -0.21875 to 0.21875
- token_mask: int32 [768], P('grp'), parts along dimension 0, may hold values from 0 to 1, as said below
Outputs:
- attended: bfloat16 [64, 384, 768], P(('grp', 'smp')), parts along dimension 0
- grad_pair: bfloat16 [768, 384, 128], P(('grp', 'smp')), parts along dimension 0
- grad_projection: float32 [256, 16], P('grp'), parts along dimension 0
The draws below stay inside these ranges and needn't reach their ends.
There are 2 independent parts, one for each index of `grp`. The reference program is written for one: setup_inputs(seed, part) draws one part's arguments, and reference() takes and returns one part's arrays. A program takes and returns all parts, laid end to end along the dimension named above; an argument that names none is the same for every part. Nothing has to cross between parts.
Inputs may be any that keep to these rules, and one draw needn't show every extreme that they name: `token_mask`: position 0 is always 1.
All inputs are finite; a program needn't handle non-finite values.
Results may differ from the reference program's by a relative error of at most 0.0045.
The reference program's roundings to bfloat16 on the way (of `bias`, `queries`, `weights`, `mixed` and `d_mixed`) count: a program that leaves them out, or rounds other values in their place, can miss the bound.
Values may be sent and summed in bfloat16 or wider, within the bound.
No kernel may reach another device: no remote copies, remote signals or barrier semaphores. Data moves between devices by JAX's collectives and lax.ppermute only.
A program may use at most 192 MiB of HBM per device.

```python
import jax
import jax.numpy as jnp
from jax import lax

D = 768
HEADS = 16
HEAD_DIM = 48
CZ = 128
NTOK = 384
SAMPLES = 32


def draw_activations(key, part):
    key = jax.random.fold_in(key, 11)
    key_base = jax.random.fold_in(key, 0)
    sample_shape = (SAMPLES, NTOK, D)
    return jnp.clip(jax.random.normal(key_base, sample_shape, jnp.float32), -6.0, 6.0).astype(jnp.bfloat16)


def draw_token_mask(key, part):
    key = jax.random.fold_in(key, 23)
    key_len, key_keep = jax.random.split(key)
    length = jax.random.randint(key_len, (), NTOK // 2, NTOK + 1)
    kept_tokens = jax.random.randint(key_keep, (NTOK,), 0, 8) > 0
    positions = jnp.arange(NTOK)
    return ((positions < length) & (kept_tokens | (positions == 0))).astype(jnp.int32)


def spiked(result, key, source, target, blocks, factor):
    def block_of(position):
        return (jnp.arange(result.shape[position]) // (result.shape[position] // blocks)).reshape((-1,) + (1,) * (result.ndim - 1 - position))

    first = jax.random.permutation(key, blocks)[block_of(target)]
    other_side = (block_of(target) + blocks // 2) % blocks
    return jnp.where((block_of(source) == first) | (block_of(source) == other_side), factor * result, result)


def steps_of(key, shape, pieces, least, top_value):
    level, own = 1.0, jax.random.fold_in(key, 6)
    for position, shards_of in pieces:
        draws = jnp.exp(jax.random.uniform(jax.random.fold_in(own, position), (shards_of,), jnp.float32, least / len(pieces), top_value / len(pieces)))
        level = level * jnp.repeat(draws, shape[position] // shards_of).reshape([-1 if axis == position else 1 for axis in range(len(shape))])
    return level


def gaussian(key, extent, deviation, reach, cuts=(), kind=jnp.bfloat16):
    result = deviation * jax.random.normal(key, extent, jnp.float32)
    if cuts:
        result = result * steps_of(key, extent, cuts, -0.22, 0.18)
    return jnp.clip(result, -reach, reach).astype(kind)


def gaussian_with(rng, dims, scale, most, shards, heavy, dtype=jnp.bfloat16):
    array = scale * jax.random.normal(rng, dims, jnp.float32)
    if shards:
        array = array * steps_of(rng, dims, shards, -0.22, 0.18)
    return jnp.clip(spiked(array, jax.random.fold_in(rng, 3), *heavy), -most, most).astype(dtype)


def setup_inputs(seed: int = 0, part: int = 0) -> dict:
    key_of = jax.random.split(jax.random.key(seed), 11)
    own_keys = jax.random.split(jax.random.fold_in(key_of[10], part), 11)
    activations = draw_activations(jax.random.fold_in(jax.random.fold_in(key_of[10], part), 71), part)
    cotangent = gaussian_with(own_keys[1], (SAMPLES, NTOK, D), 1.0, 6.0, ((0, 16),), (0, 1, 16, 2.0))
    pair_rep = gaussian(own_keys[2], (NTOK, NTOK, CZ), 1.0, 6.0, ((0, 16),))
    pair_gain = jnp.clip(1.0 + 0.1 * jax.random.normal(key_of[3], (CZ,), jnp.float32), 0.5, 1.5)
    w_pair = gaussian(key_of[4], (CZ, HEADS), CZ ** -0.5, 0.5)
    w_query = gaussian(key_of[5], (D, D), D ** -0.5, 0.21875)
    w_key = gaussian(key_of[6], (D, D), D ** -0.5, 0.21875)
    w_value = gaussian(key_of[7], (D, D), D ** -0.5, 0.21875)
    w_out = gaussian(key_of[8], (D, D), D ** -0.5, 0.21875)
    token_mask = draw_token_mask(jax.random.fold_in(jax.random.fold_in(key_of[10], part), 71), part)
    return {"activations": activations, "cotangent": cotangent, "pair_rep": pair_rep, "pair_gain": pair_gain, "w_pair": w_pair, "w_query": w_query, "w_key": w_key, "w_value": w_value, "w_out": w_out, "token_mask": token_mask}


def normalize(pair_rep, pair_gain):
    values_f = pair_rep.astype(jnp.float32)
    centre = lax.optimization_barrier(jnp.mean(values_f, axis=-1, keepdims=True))
    spread = lax.optimization_barrier(jnp.mean((values_f - centre) ** 2, axis=-1, keepdims=True))
    rstd = lax.rsqrt(spread + 1e-05)
    centred = (values_f - centre) * rstd
    return (centred * pair_gain, centred, rstd)

def sample_pass(sample_act, sample_cot, bias, live_keys, w_query, w_key, w_value, w_out):

    def project(weight):
        return jnp.dot(sample_act, weight, preferred_element_type=jnp.float32).astype(jnp.bfloat16).reshape(NTOK, HEADS, HEAD_DIM)
    queries = project(w_query)
    keys_proj = project(w_key)
    values_proj = project(w_value)
    scores = jnp.einsum('ihd,jhd->ihj', queries.astype(jnp.float32), keys_proj.astype(jnp.float32)) * HEAD_DIM ** (-0.5) + bias.astype(jnp.float32)
    scores = jnp.where(live_keys[None, None, :], scores, -1e+30)
    row_top = lax.optimization_barrier(jnp.max(scores, axis=-1, keepdims=True))
    exps = jnp.exp(scores - row_top)
    probs = exps / lax.optimization_barrier(jnp.sum(exps, axis=-1, keepdims=True))
    weights = probs.astype(jnp.bfloat16)
    mixed = jnp.einsum('ihj,jhd->ihd', weights.astype(jnp.float32), values_proj.astype(jnp.float32)).astype(jnp.bfloat16).reshape(NTOK, D)
    output = jnp.dot(mixed, w_out, preferred_element_type=jnp.float32)
    output = jnp.where(live_keys[:, None], output, 0.0).astype(jnp.bfloat16)
    masked_cot = jnp.where(live_keys[:, None], sample_cot, jnp.zeros_like(sample_cot))
    d_mixed = jnp.dot(masked_cot, w_out.T, preferred_element_type=jnp.float32).astype(jnp.bfloat16).reshape(NTOK, HEADS, HEAD_DIM)
    d_probs = jnp.einsum('ihd,jhd->ihj', d_mixed.astype(jnp.float32), values_proj.astype(jnp.float32))
    row_delta = lax.optimization_barrier(jnp.sum(probs * d_probs, axis=-1, keepdims=True))
    return (output, probs * (d_probs - row_delta))

def reference(activations, cotangent, pair_rep, pair_gain, w_pair, w_query, w_key, w_value, w_out, token_mask):
    normed, centred, rstd = normalize(pair_rep, pair_gain)
    bias = jnp.einsum('ijc,ch->ihj', normed, w_pair.astype(jnp.float32), precision=lax.Precision.HIGHEST).astype(jnp.bfloat16)
    live_keys = token_mask > 0

    def one_sample(grad_total, item):
        output, d_scores = sample_pass(item[0], item[1], bias, live_keys, w_query, w_key, w_value, w_out)
        return (grad_total + d_scores, output)
    bias_grad, attended = lax.scan(one_sample, jnp.zeros((NTOK, HEADS, NTOK), jnp.float32), (activations, cotangent))
    grad_projection = jnp.einsum('ijc,ihj->ch', normed, bias_grad, precision=lax.Precision.HIGHEST)
    d_normed = jnp.einsum('ihj,ch->ijc', bias_grad, w_pair.astype(jnp.float32), precision=lax.Precision.HIGHEST) * pair_gain
    first_mean = lax.optimization_barrier(jnp.mean(d_normed, axis=-1, keepdims=True))
    second_mean = lax.optimization_barrier(jnp.mean(d_normed * centred, axis=-1, keepdims=True))
    grad_pair = (rstd * (d_normed - first_mean - centred * second_mean)).astype(jnp.bfloat16)
    return (attended, grad_pair, grad_projection)
```

```python
import functools
import math

import jax
import jax.numpy as jnp
from jax import lax
from jax.experimental import pallas as pl
from jax.experimental.pallas import tpu as pltpu
from jax.sharding import PartitionSpec as P

F32 = jnp.float32
BF16 = jnp.bfloat16
LOG2E = math.log2(math.e)
NT = (((1,), (1,)), ((), ()))
TN = (((0,), (0,)), ((), ()))
VMEM_LIMIT = 48 * 1024 * 1024
HEAD_CHUNKS = 2
ROW_STEP = 128


def normalize(pair_rep, pair_gain):
    values_f = pair_rep.astype(F32)
    centre = jnp.mean(values_f, axis=-1, keepdims=True)
    spread = jnp.mean((values_f - centre) ** 2, axis=-1, keepdims=True)
    rstd = lax.rsqrt(spread + 1e-05)
    centred = (values_f - centre) * rstd
    return (centred * pair_gain, centred, rstd)


def per_device_plain(
    activations, cotangent, pair_rep, pair_gain, w_pair, w_query, w_key, w_value, w_out, token_mask
):
    head_count = w_pair.shape[1]
    model_width = w_query.shape[0]
    head_width = model_width // head_count
    tok_count = token_mask.shape[0]
    normed, centred, rstd = normalize(pair_rep, pair_gain)
    bias_rows = jnp.einsum(
        "rjc,ch->rhj", normed, w_pair.astype(F32), precision=lax.Precision.HIGHEST
    ).astype(BF16)
    bias_full = lax.all_gather(bias_rows, "smp", axis=0, tiled=True).astype(F32)
    live_keys = token_mask > 0
    outputs = []
    grad_total = None
    for sample_index in range(activations.shape[0]):
        sample_act = activations[sample_index]

        def project(weight):
            return (
                jnp.dot(sample_act, weight, preferred_element_type=F32)
                .astype(BF16)
                .reshape(tok_count, head_count, head_width)
            )

        queries, keys_proj, values_proj = project(w_query), project(w_key), project(w_value)
        scores = (
            jnp.einsum("ihd,jhd->ihj", queries, keys_proj, preferred_element_type=F32)
            * head_width ** (-0.5)
            + bias_full
        )
        scores = jnp.where(live_keys[None, None, :], scores, -1e30)
        exps = jnp.exp(scores - jnp.max(scores, axis=-1, keepdims=True))
        probs = exps / jnp.sum(exps, axis=-1, keepdims=True)
        mixed = (
            jnp.einsum("ihj,jhd->ihd", probs.astype(BF16), values_proj, preferred_element_type=F32)
            .astype(BF16)
            .reshape(tok_count, model_width)
        )
        output = jnp.dot(mixed, w_out, preferred_element_type=F32)
        outputs.append(jnp.where(live_keys[:, None], output, 0.0).astype(BF16))
        sample_cot = cotangent[sample_index]
        masked_cot = jnp.where(live_keys[:, None], sample_cot, jnp.zeros_like(sample_cot))
        d_mixed = (
            jnp.dot(masked_cot, w_out.T, preferred_element_type=F32)
            .astype(BF16)
            .reshape(tok_count, head_count, head_width)
        )
        d_probs = jnp.einsum("ihd,jhd->ihj", d_mixed, values_proj, preferred_element_type=F32)
        d_scores = probs * (d_probs - jnp.sum(probs * d_probs, axis=-1, keepdims=True))
        grad_total = d_scores if grad_total is None else grad_total + d_scores
    bias_grad = lax.psum_scatter(grad_total, "smp", scatter_dimension=0, tiled=True)
    proj_local = jnp.einsum("rjc,rhj->ch", normed, bias_grad, precision=lax.Precision.HIGHEST)
    grad_projection = lax.psum(proj_local, "smp")
    d_normed = (
        jnp.einsum("rhj,ch->rjc", bias_grad, w_pair.astype(F32), precision=lax.Precision.HIGHEST)
        * pair_gain
    )
    first_mean = jnp.mean(d_normed, axis=-1, keepdims=True)
    second_mean = jnp.mean(d_normed * centred, axis=-1, keepdims=True)
    grad_pair = (rstd * (d_normed - first_mean - centred * second_mean)).astype(BF16)
    return (jnp.stack(outputs), grad_pair, grad_projection)


def dot(left, right, dims=None):
    if dims is None:
        return jnp.dot(left, right, preferred_element_type=F32)
    return lax.dot_general(left, right, dims, preferred_element_type=F32)


def pieces3(value):
    high = value.astype(BF16)
    rest = value - high.astype(F32)
    mid = rest.astype(BF16)
    low = (rest - mid.astype(F32)).astype(BF16)
    return high, mid, low


def bias_kernel(core_ref, pair_ref, gain_ref, wt_ref, mask_ref, own_ref, other_ref, mean_ref, rstd_ref, held):
    rows, tok, chan = pair_ref.shape
    heads = wt_ref.shape[0]
    half = heads // 2
    scaled = wt_ref[...].astype(F32) * gain_ref[...]
    total = jnp.sum(scaled, axis=1, keepdims=True)
    left = jnp.concatenate([*pieces3(scaled), jnp.ones((16, chan), BF16)], axis=0)
    ones_c = jnp.ones((chan, chan), BF16)
    ones_r = jnp.ones((8, 3 * chan), BF16)
    live = mask_ref[...] > 0
    for i in range(rows):
        values = pair_ref[i]
        sums = dot(left, values, NT)
        mean_row = sums[3 * heads : 3 * heads + 1] * (1.0 / chan)
        diff = values.astype(F32) - dot(values, ones_c) * (1.0 / chan)
        squares = jnp.concatenate(pieces3(diff * diff), axis=1)
        spread = dot(ones_r, squares, NT)[0:1] * (1.0 / chan)
        rstd_row = lax.rsqrt(spread + 1e-05)
        raw = sums[0:heads] + (sums[heads : 2 * heads] + sums[2 * heads : 3 * heads])
        bias = (raw - total * mean_row) * rstd_row
        bias = jnp.where(live, bias, -1e30)
        held[:, i, :] = bias
        mean_ref[i : i + 1, :] = mean_row
        rstd_ref[i : i + 1, :] = rstd_row
    core = core_ref[0]
    own_ref[...] = held[pl.ds(core * half, half)].astype(BF16)
    other_ref[...] = held[pl.ds((1 - core) * half, half)].astype(BF16)


def bias_call(core, pair_rep, gain, w_t, mask_row):
    rows, tok, chan = pair_rep.shape
    heads = w_t.shape[0]
    half = heads // 2
    vm = pl.BlockSpec(memory_space=pltpu.VMEM)
    return pl.pallas_call(
        bias_kernel,
        out_shape=[
            jax.ShapeDtypeStruct((half, rows, tok), BF16),
            jax.ShapeDtypeStruct((half, rows, tok), BF16),
            jax.ShapeDtypeStruct((rows, tok), F32),
            jax.ShapeDtypeStruct((rows, tok), F32),
        ],
        in_specs=[pl.BlockSpec(memory_space=pltpu.SMEM)] + [vm] * 4,
        out_specs=[vm] * 4,
        scratch_shapes=[pltpu.VMEM((heads, rows, tok), F32)],
        compiler_params=pltpu.CompilerParams(vmem_limit_bytes=VMEM_LIMIT),
        cost_estimate=pl.CostEstimate(flops=int(6e9), bytes_accessed=int(4e6), transcendentals=0),
        name="pair_bias",
    )(core, pair_rep, gain, w_t, mask_row)


def project_kernel(core_ref, act_ref, cot_ref, wq_ref, wk_ref, wv_ref, wo_ref, mask_ref, q_ref, k_ref, v_ref, d_ref):
    act = act_ref[0]
    for weight, out in ((wq_ref, q_ref), (wk_ref, k_ref), (wv_ref, v_ref)):
        out[0] = dot(act, weight[...]).T.astype(BF16)
    live = mask_ref[...] > 0
    d_ref[0] = jnp.where(live, dot(wo_ref[...], cot_ref[0], NT), 0.0).astype(BF16)


def project_call(core, act, cot, w_query, w_key, w_value, w_out, mask_row):
    samples, tok, width = act.shape
    half = width // 2
    columns = pl.BlockSpec((width, half), lambda s, c: (0, c[0]))
    per_sample = pl.BlockSpec((1, tok, width), lambda s, c: (s, 0, 0))
    out = pl.BlockSpec((1, half, tok), lambda s, c: (s, 0, 0))
    return pl.pallas_call(
        project_kernel,
        grid_spec=pltpu.PrefetchScalarGridSpec(
            num_scalar_prefetch=1,
            grid=(samples,),
            in_specs=[per_sample, per_sample, columns, columns, columns,
                      pl.BlockSpec((half, width), lambda s, c: (c[0], 0)),
                      pl.BlockSpec((1, tok), lambda s, c: (0, 0))],
            out_specs=[out] * 4,
        ),
        out_shape=[jax.ShapeDtypeStruct((samples, half, tok), BF16)] * 4,
        compiler_params=pltpu.CompilerParams(vmem_limit_bytes=VMEM_LIMIT),
        cost_estimate=pl.CostEstimate(
            flops=8 * samples * tok * width * half, bytes_accessed=int(6e6), transcendentals=0
        ),
        name="projections",
    )(core, act, cot, w_query, w_key, w_value, w_out, mask_row)


def code16(block):
    top = jnp.max(jnp.abs(block), axis=0, keepdims=True)
    inverse = jnp.where(top > 0, 32766.0 / jnp.where(top > 0, top, 1.0), 0.0)
    codes = jnp.round(block * inverse).astype(jnp.int32).astype(jnp.int16)
    return codes, top * (1.0 / 32766.0)


def decode16(codes, scale):
    return codes.astype(jnp.int32).astype(F32) * scale


def attention_kernel(za, yb, head_width, offs_ref, *refs):
    slots = za * yb
    bias_refs = refs[:slots]
    q0, k0, v0, d0, q1, k1, v1, d1 = refs[slots : slots + 8]
    mixed0, mixed1, own_ref, code_ref, scale_ref, bias_f, grad = refs[slots + 8 :]
    tok = bias_f.shape[0]
    part = bias_refs[0].shape[1] // 2
    for slot in range(slots):
        block = bias_refs[slot][0].astype(F32) * LOG2E
        for side in range(2):
            start = pl.multiple_of(offs_ref[slot * 2 + side], 8)
            bias_f[pl.ds(start, part), :] = block[side * part : (side + 1) * part]
    factor = head_width ** (-0.5) * LOG2E
    count = q0.shape[0]
    for s in range(2 * count):
        qr, kr, vr, dr, mr = (q0, k0, v0, d0, mixed0) if s < count else (q1, k1, v1, d1, mixed1)
        at = s % count
        query, key_t, value_t, dmix = qr[at].T, kr[at], vr[at], dr[at].T
        value = value_t.T
        for r in range(0, tok, ROW_STEP):
            rows = slice(r, r + ROW_STEP)
            scores = dot(query[rows], key_t) * factor + bias_f[rows, :]
            top = jnp.max(scores, axis=1, keepdims=True)
            exps = jnp.exp2(scores - top)
            probs = exps * (1.0 / jnp.sum(exps, axis=1, keepdims=True))
            mixed = dot(probs.astype(BF16), value)
            mr[at, :, rows] = mixed.T.astype(BF16)
            d_probs = dot(dmix[rows], value_t)
            delta = jnp.sum(probs * d_probs, axis=1, keepdims=True)
            d_scores = probs * (d_probs - delta)
            if s == 0:
                grad[rows, :] = d_scores
            else:
                grad[rows, :] += d_scores
    for ky in range(yb):
        for kz in range(za):
            at = 2 * slots + (ky * za + kz) * 2
            block = jnp.concatenate(
                [grad[pl.ds(pl.multiple_of(offs_ref[at + side], 8), part), :] for side in range(2)], axis=0
            )
            if ky == 0:
                own_ref[kz, 0] = block
            else:
                codes, scale = code16(block)
                code_ref[ky - 1, kz, 0] = codes
                scale_ref[ky - 1, kz, 0] = scale


def attention_call(za, yb, head_width, offsets, bias_slots, first, own_proj, sib_proj):
    chunk, rows, tok = bias_slots[0].shape
    count = own_proj[0].shape[0]
    slots = za * yb
    head = pl.BlockSpec((count, head_width, tok), lambda h, o: (0, first + h, 0))
    mixed = pl.BlockSpec((count, head_width, tok), lambda h, o: (0, h, 0))
    away = max(yb - 1, 1)
    tiles = 2 * count * chunk
    return pl.pallas_call(
        functools.partial(attention_kernel, za, yb, head_width),
        grid_spec=pltpu.PrefetchScalarGridSpec(
            num_scalar_prefetch=1,
            grid=(chunk,),
            in_specs=[pl.BlockSpec((1, rows, tok), lambda h, o: (h, 0, 0))] * slots + [head] * 8,
            out_specs=[
                mixed,
                mixed,
                pl.BlockSpec((za, 1, rows, tok), lambda h, o: (0, h, 0, 0)),
                pl.BlockSpec((away, za, 1, rows, tok), lambda h, o: (0, 0, h, 0, 0)),
                pl.BlockSpec((away, za, 1, 1, tok), lambda h, o: (0, 0, h, 0, 0)),
            ],
            scratch_shapes=[pltpu.VMEM((tok, tok), F32), pltpu.VMEM((tok, tok), F32)],
        ),
        out_shape=[
            jax.ShapeDtypeStruct((count, chunk * head_width, tok), BF16),
            jax.ShapeDtypeStruct((count, chunk * head_width, tok), BF16),
            jax.ShapeDtypeStruct((za, chunk, rows, tok), F32),
            jax.ShapeDtypeStruct((away, za, chunk, rows, tok), jnp.int16),
            jax.ShapeDtypeStruct((away, za, chunk, 1, tok), F32),
        ],
        compiler_params=pltpu.CompilerParams(vmem_limit_bytes=VMEM_LIMIT),
        cost_estimate=pl.CostEstimate(
            flops=tiles * 6 * tok * tok * 256, bytes_accessed=int(8e6), transcendentals=tiles * tok * tok
        ),
        name="attention",
    )(offsets, *bias_slots, *own_proj, *sib_proj)


def join_kernel(za, yb, own_ref, code_ref, scale_ref, stay_ref, next_code_ref, next_scale_ref):
    for kz in range(za):
        block = own_ref[kz, 0]
        for ky in range(yb - 1):
            block = block + decode16(code_ref[ky, kz, 0], scale_ref[ky, kz, 0])
        if kz == 0:
            stay_ref[0] = block
        else:
            codes, scale = code16(block)
            next_code_ref[kz - 1, 0] = codes
            next_scale_ref[kz - 1, 0] = scale


def join_call(own, codes, scales):
    za, chunk, rows, tok = own.shape
    away = codes.shape[0]
    return pl.pallas_call(
        functools.partial(join_kernel, za, away + 1),
        grid=(chunk,),
        in_specs=[
            pl.BlockSpec((za, 1, rows, tok), lambda h: (0, h, 0, 0)),
            pl.BlockSpec((away, za, 1, rows, tok), lambda h: (0, 0, h, 0, 0)),
            pl.BlockSpec((away, za, 1, 1, tok), lambda h: (0, 0, h, 0, 0)),
        ],
        out_specs=[
            pl.BlockSpec((1, rows, tok), lambda h: (h, 0, 0)),
            pl.BlockSpec((za - 1, 1, rows, tok), lambda h: (0, h, 0, 0)),
            pl.BlockSpec((za - 1, 1, 1, tok), lambda h: (0, h, 0, 0)),
        ],
        out_shape=[
            jax.ShapeDtypeStruct((chunk, rows, tok), F32),
            jax.ShapeDtypeStruct((za - 1, chunk, rows, tok), jnp.int16),
            jax.ShapeDtypeStruct((za - 1, chunk, 1, tok), F32),
        ],
        compiler_params=pltpu.CompilerParams(vmem_limit_bytes=VMEM_LIMIT),
        cost_estimate=pl.CostEstimate(flops=int(4e6), bytes_accessed=int(6e6), transcendentals=0),
        name="join_y",
    )(own, codes, scales)


def total_kernel(count, *refs):
    stay_ref = refs[0]
    code_refs, scale_refs = refs[1 : 1 + count], refs[1 + count : 1 + 2 * count]
    own_ref, sib_ref = refs[1 + 2 * count :]
    part = own_ref.shape[1]
    block = stay_ref[0]
    for codes, scale in zip(code_refs, scale_refs):
        block = block + decode16(codes[0], scale[0])
    own_ref[0] = block[:part]
    sib_ref[0] = block[part:]


def total_call(stay, codes, scales):
    chunk, rows, tok = stay.shape
    block = pl.BlockSpec((1, rows, tok), lambda h: (h, 0, 0))
    row = pl.BlockSpec((1, 1, tok), lambda h: (h, 0, 0))
    out = pl.BlockSpec((1, rows // 2, tok), lambda h: (h, 0, 0))
    return pl.pallas_call(
        functools.partial(total_kernel, len(codes)),
        grid=(chunk,),
        in_specs=[block] * (1 + len(codes)) + [row] * len(scales),
        out_specs=[out, out],
        out_shape=[jax.ShapeDtypeStruct((chunk, rows // 2, tok), F32)] * 2,
        compiler_params=pltpu.CompilerParams(vmem_limit_bytes=VMEM_LIMIT),
        cost_estimate=pl.CostEstimate(flops=int(2e6), bytes_accessed=int(3e6), transcendentals=0),
        name="join_z",
    )(stay, *codes, *scales)


def output_kernel(parts, core_ref, *refs):
    own_refs, other_refs = refs[:parts], refs[parts : 2 * parts]
    w_own, w_other, mask_ref, out_ref = refs[2 * parts :]
    live = mask_ref[...] > 0
    total = None
    for group, weight in ((own_refs, w_own), (other_refs, w_other)):
        start = 0
        for ref in group:
            size = ref.shape[1]
            mixed = ref[0]
            mixed = jnp.where(live, mixed.astype(F32), 0.0).T.astype(BF16)
            term = dot(mixed, weight[start : start + size, :])
            total = term if total is None else total + term
            start += size
    out_ref[0] = total.astype(BF16)


def output_call(core, own, other, w_out, mask_row):
    samples, size, tok = own[0].shape
    parts = len(own)
    width = w_out.shape[0]
    half = width // 2
    block = pl.BlockSpec((1, size, tok), lambda s, c: (s, 0, 0))
    return pl.pallas_call(
        functools.partial(output_kernel, parts),
        grid_spec=pltpu.PrefetchScalarGridSpec(
            num_scalar_prefetch=1,
            grid=(samples,),
            in_specs=[block] * (2 * parts)
            + [
                pl.BlockSpec((half, width), lambda s, c: (c[0], 0)),
                pl.BlockSpec((half, width), lambda s, c: (1 - c[0], 0)),
                pl.BlockSpec((1, tok), lambda s, c: (0, 0)),
            ],
            out_specs=pl.BlockSpec((1, tok, width), lambda s, c: (s, 0, 0)),
        ),
        out_shape=jax.ShapeDtypeStruct((samples, tok, width), BF16),
        compiler_params=pltpu.CompilerParams(vmem_limit_bytes=VMEM_LIMIT),
        cost_estimate=pl.CostEstimate(
            flops=2 * samples * tok * width * width, bytes_accessed=int(4e6), transcendentals=0
        ),
        name="output",
    )(core, *own, *other, w_out, w_out, mask_row)


def load_rows(refs, i):
    return jnp.concatenate([ref[:, i, :] for ref in refs], axis=0)


def projection_kernel(parts, core_ref, *refs):
    own_refs, other_refs = refs[:parts], refs[parts : 2 * parts]
    pair_ref, gain_ref, mean_ref, rstd_ref, out_ref = refs[2 * parts :]
    rows, tok, chan = pair_ref.shape
    heads = out_ref.shape[0]
    half = heads // 2
    total = jnp.zeros((3 * heads, chan), F32)
    means = jnp.zeros((heads, tok), F32)
    for i in range(rows):
        grads = load_rows([*own_refs, *other_refs], i) * rstd_ref[i : i + 1, :]
        means = means + grads * mean_ref[i : i + 1, :]
        total = total + dot(jnp.concatenate(pieces3(grads), axis=0), pair_ref[i])
    raw = total[:heads] + (total[heads : 2 * heads] + total[2 * heads :])
    result = (raw - jnp.sum(means, axis=1, keepdims=True)) * gain_ref[...]
    core = core_ref[0]
    out_ref[pl.ds(pl.multiple_of(core * half, half), half), :] = result[:half]
    out_ref[pl.ds(pl.multiple_of((1 - core) * half, half), half), :] = result[half:]


def pair_grad_kernel(parts, core_ref, *refs):
    own_refs, other_refs = refs[:parts], refs[parts : 2 * parts]
    pair_ref, gain_ref, wt_ref, rstd_ref, out_ref = refs[2 * parts :]
    rows, tok, chan = pair_ref.shape
    half = wt_ref.shape[0] // 2
    core = core_ref[0]
    weights = jnp.concatenate(
        [
            wt_ref[pl.ds(pl.multiple_of(core * half, half), half), :],
            wt_ref[pl.ds(pl.multiple_of((1 - core) * half, half), half), :],
        ],
        axis=0,
    )
    scaled = weights * gain_ref[...]
    scaled = scaled - jnp.mean(scaled, axis=1, keepdims=True)
    wh, wm, wl = pieces3(scaled)
    right = jnp.concatenate([wh, wm, wh, wl, wm, wh], axis=0)
    for i in range(rows):
        grads = load_rows([*own_refs, *other_refs], i) * rstd_ref[i : i + 1, :]
        gh, gm, gl = pieces3(grads)
        left = jnp.concatenate([gh, gh, gm, gh, gm, gl], axis=0)
        slope = dot(left, right, TN)
        values = pair_ref[i].astype(F32)
        diff = values - jnp.sum(values, axis=1, keepdims=True) * (1.0 / chan)
        spread = jnp.sum(diff * diff, axis=1, keepdims=True) * (1.0 / chan)
        along = jnp.sum(slope * diff, axis=1, keepdims=True) * (1.0 / chan)
        out_ref[i] = (slope - diff * (along / (spread + 1e-05))).astype(BF16)


def final_call(kernel, name, core, own, other, operands, out_shape):
    vm = pl.BlockSpec(memory_space=pltpu.VMEM)
    parts = len(own)
    return pl.pallas_call(
        functools.partial(kernel, parts),
        in_specs=[pl.BlockSpec(memory_space=pltpu.SMEM)] + [vm] * (2 * parts + len(operands)),
        out_specs=vm,
        out_shape=out_shape,
        compiler_params=pltpu.CompilerParams(vmem_limit_bytes=VMEM_LIMIT),
        cost_estimate=pl.CostEstimate(flops=int(4e9), bytes_accessed=int(8e6), transcendentals=0),
        name=name,
    )(core, *own, *other, *operands)


def grid_of(devices):
    chips = devices // 2
    yb = 1 << ((chips.bit_length() - 1) // 2)
    return chips // yb, yb


def per_device_tiled(
    devices, activations, cotangent, pair_rep, pair_gain, w_pair, w_query, w_key, w_value, w_out, token_mask
):
    za, yb = grid_of(devices)
    rows, tok, chan = pair_rep.shape
    heads = w_pair.shape[1]
    half = heads // 2
    head_width = w_query.shape[0] // heads
    me = lax.axis_index("smp")
    core = lax.rem(me, 2)
    chip = me // 2
    my_z, my_y = chip // yb, lax.rem(chip, yb)

    def swap_core(x):
        return lax.ppermute(x, "smp", [(d, d ^ 1) for d in range(devices)])

    def shift(x, kz, ky):
        perm = []
        for d in range(devices):
            z, y, c = d // 2 // yb, d // 2 % yb, d % 2
            perm.append((d, (((z + kz) % za) * yb + (y + ky) % yb) * 2 + c))
        return lax.ppermute(x, "smp", perm)

    offsets = []
    for sign in (-1, 1):
        for ky in range(yb):
            for kz in range(za):
                there = lax.rem(my_z + sign * kz + za, za) * yb + lax.rem(my_y + sign * ky + yb, yb)
                offsets += [there * 2 * rows + core * rows, there * 2 * rows + (1 - core) * rows]
    offsets = jnp.stack(offsets).astype(jnp.int32)
    core_1 = core.reshape(1).astype(jnp.int32)
    gain = pair_gain.reshape(1, chan)
    w_t = w_pair.T.astype(F32)
    mask_row = token_mask.reshape(1, tok)

    sib_act, sib_cot = swap_core(activations), swap_core(cotangent)
    bias_own, bias_other, mean_rows, rstd_rows = bias_call(core_1, pair_rep, gain, w_t, mask_row)
    bias_chip = jnp.concatenate([bias_own, swap_core(bias_other)], axis=1)

    chunk = half // HEAD_CHUNKS
    slots = []
    for n in range(HEAD_CHUNKS):
        mine = bias_chip[n * chunk : (n + 1) * chunk]
        column = [mine] + [shift(mine, kz, 0) for kz in range(1, za)]
        slots.append([shift(block, 0, ky) if ky else block for ky in range(yb) for block in column])
    weights = (w_query, w_key, w_value, w_out)
    own_proj = project_call(core_1, activations, cotangent, *weights, mask_row)
    sib_proj = project_call(core_1, sib_act, sib_cot, *weights, mask_row)

    mixed_own, mixed_other, grads_own, grads_other = [], [], [], []
    for n in range(HEAD_CHUNKS):
        mixed0, mixed1, own, codes, scales = attention_call(
            za, yb, head_width, offsets, slots[n], n * chunk, own_proj, sib_proj
        )
        mixed_own.append(mixed0)
        mixed_other.append(swap_core(mixed1))
        far_codes = jnp.stack([shift(codes[ky - 1], 0, ky) for ky in range(1, yb)]) if yb > 2 else shift(codes, 0, 1)
        far_scales = jnp.stack([shift(scales[ky - 1], 0, ky) for ky in range(1, yb)]) if yb > 2 else shift(scales, 0, 1)
        stay, codes, scales = join_call(own, far_codes, far_scales)
        codes = [shift(codes[kz - 1], kz, 0) for kz in range(1, za)]
        scales = [shift(scales[kz - 1], kz, 0) for kz in range(1, za)]
        here, there = total_call(stay, codes, scales)
        grads_own.append(here)
        grads_other.append(swap_core(there))

    attended = output_call(core_1, mixed_own, mixed_other, w_out, mask_row)
    projection = final_call(
        projection_kernel, "pair_projection", core_1, grads_own, grads_other,
        (pair_rep, gain, mean_rows, rstd_rows), jax.ShapeDtypeStruct((heads, chan), F32),
    )
    step = 1
    while step < devices:
        projection = projection + lax.ppermute(projection, "smp", [(d, d ^ step) for d in range(devices)])
        step *= 2
    grad_pair = final_call(
        pair_grad_kernel, "pair_gradient", core_1, grads_own, grads_other,
        (pair_rep, gain, w_t, rstd_rows), jax.ShapeDtypeStruct(pair_rep.shape, BF16),
    )
    return (attended, grad_pair, projection.T)


def per_device(devices, activations, *rest):
    pair_rep, w_pair = rest[1], rest[3]
    rows, heads = pair_rep.shape[0], w_pair.shape[1]
    power = devices >= 8 and devices & (devices - 1) == 0
    if power and rows % 8 == 0 and heads % (2 * HEAD_CHUNKS) == 0 and pair_rep.shape[1] % ROW_STEP == 0:
        return per_device_tiled(devices, activations, *rest)
    return per_device_plain(activations, *rest)


def solution(mesh):
    split = P(("grp", "smp"), None, None)
    return jax.shard_map(
        functools.partial(per_device, mesh.shape["smp"]),
        mesh=mesh,
        in_specs=(split, split, split, P(), P(), P(), P(), P(), P(), P("grp")),
        out_specs=(split, split, P("grp", None)),
        check_vma=False,
    )
```

```python
import functools
import math

import jax
import jax.numpy as jnp
from jax import lax
from jax.experimental import pallas as pl
from jax.experimental.pallas import tpu as pltpu
from jax.sharding import Mesh
from jax.sharding import PartitionSpec as P

F32 = jnp.float32
BF16 = jnp.bfloat16
LOG2E = math.log2(math.e)
NT = (((1,), (1,)), ((), ()))
TN = (((0,), (0,)), ((), ()))
VMEM_LIMIT = 48 * 1024 * 1024
CHUNKS = ((4, True), (4, True))


def normalize(pair_rep, pair_gain):
    values_f = pair_rep.astype(F32)
    centre = jnp.mean(values_f, axis=-1, keepdims=True)
    spread = jnp.mean((values_f - centre) ** 2, axis=-1, keepdims=True)
    rstd = lax.rsqrt(spread + 1e-05)
    centred = (values_f - centre) * rstd
    return (centred * pair_gain, centred, rstd)


def per_device_plain(
    activations, cotangent, pair_rep, pair_gain, w_pair, w_query, w_key, w_value, w_out, token_mask
):
    head_count = w_pair.shape[1]
    model_width = w_query.shape[0]
    head_width = model_width // head_count
    tok_count = token_mask.shape[0]
    normed, centred, rstd = normalize(pair_rep, pair_gain)
    bias_rows = jnp.einsum(
        "rjc,ch->rhj", normed, w_pair.astype(F32), precision=lax.Precision.HIGHEST
    ).astype(BF16)
    bias_full = lax.all_gather(bias_rows, "smp", axis=0, tiled=True).astype(F32)
    live_keys = token_mask > 0
    outputs = []
    grad_total = None
    for sample_index in range(activations.shape[0]):
        sample_act = activations[sample_index]

        def project(weight):
            return (
                jnp.dot(sample_act, weight, preferred_element_type=F32)
                .astype(BF16)
                .reshape(tok_count, head_count, head_width)
            )

        queries, keys_proj, values_proj = project(w_query), project(w_key), project(w_value)
        scores = (
            jnp.einsum("ihd,jhd->ihj", queries, keys_proj, preferred_element_type=F32)
            * head_width ** (-0.5)
            + bias_full
        )
        scores = jnp.where(live_keys[None, None, :], scores, -1e30)
        exps = jnp.exp(scores - jnp.max(scores, axis=-1, keepdims=True))
        probs = exps / jnp.sum(exps, axis=-1, keepdims=True)
        mixed = (
            jnp.einsum("ihj,jhd->ihd", probs.astype(BF16), values_proj, preferred_element_type=F32)
            .astype(BF16)
            .reshape(tok_count, model_width)
        )
        output = jnp.dot(mixed, w_out, preferred_element_type=F32)
        outputs.append(jnp.where(live_keys[:, None], output, 0.0).astype(BF16))
        sample_cot = cotangent[sample_index]
        masked_cot = jnp.where(live_keys[:, None], sample_cot, jnp.zeros_like(sample_cot))
        d_mixed = (
            jnp.dot(masked_cot, w_out.T, preferred_element_type=F32)
            .astype(BF16)
            .reshape(tok_count, head_count, head_width)
        )
        d_probs = jnp.einsum("ihd,jhd->ihj", d_mixed, values_proj, preferred_element_type=F32)
        d_scores = probs * (d_probs - jnp.sum(probs * d_probs, axis=-1, keepdims=True))
        grad_total = d_scores if grad_total is None else grad_total + d_scores
    bias_grad = lax.psum_scatter(grad_total, "smp", scatter_dimension=0, tiled=True)
    proj_local = jnp.einsum("rjc,rhj->ch", normed, bias_grad, precision=lax.Precision.HIGHEST)
    grad_projection = lax.psum(proj_local, "smp")
    d_normed = (
        jnp.einsum("rhj,ch->rjc", bias_grad, w_pair.astype(F32), precision=lax.Precision.HIGHEST)
        * pair_gain
    )
    first_mean = jnp.mean(d_normed, axis=-1, keepdims=True)
    second_mean = jnp.mean(d_normed * centred, axis=-1, keepdims=True)
    grad_pair = (rstd * (d_normed - first_mean - centred * second_mean)).astype(BF16)
    return (jnp.stack(outputs), grad_pair, grad_projection)


def dot(left, right, dims=None):
    if dims is None:
        return jnp.dot(left, right, preferred_element_type=F32)
    return lax.dot_general(left, right, dims, preferred_element_type=F32)


def pieces3(value):
    high = value.astype(BF16)
    rest = value - high.astype(F32)
    mid = rest.astype(BF16)
    low = (rest - mid.astype(F32)).astype(BF16)
    return high, mid, low


def bias_kernel(core_ref, pair_ref, gain_ref, wt_ref, mask_ref, own_ref, other_ref, mean_ref, rstd_ref, held):
    rows, tok, chan = pair_ref.shape
    heads = wt_ref.shape[0]
    half = heads // 2
    scaled = wt_ref[...] * gain_ref[...]
    total = jnp.sum(scaled, axis=1, keepdims=True)
    left = jnp.concatenate([*pieces3(scaled), jnp.ones((16, chan), BF16)], axis=0)
    lane = lax.broadcasted_iota(jnp.int32, (tok, 128), 1)
    spreads = jnp.zeros((tok, 128), F32)
    for i in range(rows):
        values = pair_ref[i].astype(F32)
        diff = values - jnp.sum(values, axis=1, keepdims=True) * (1.0 / chan)
        spread = jnp.sum(diff * diff, axis=1, keepdims=True) * (1.0 / chan)
        spreads = jnp.where(lane == i, spread, spreads)
    rstd = lax.rsqrt(spreads.T[:rows] + 1e-05)
    rstd_ref[...] = rstd
    for i in range(rows):
        sums = dot(left, pair_ref[i], NT)
        mean_row = sums[3 * heads : 3 * heads + 1] * (1.0 / chan)
        raw = sums[0:heads] + (sums[heads : 2 * heads] + sums[2 * heads : 3 * heads])
        held[:, i, :] = (raw - total * mean_row) * rstd[i : i + 1]
        mean_ref[i : i + 1, :] = mean_row
    core = core_ref[0]
    live = (mask_ref[...] > 0)[None]
    own_ref[...] = jnp.where(live, held[pl.ds(core * half, half)], -1e30).astype(BF16)
    other_ref[...] = jnp.where(live, held[pl.ds((1 - core) * half, half)], -1e30).astype(BF16)


def bias_call(core, pair_rep, gain, w_t, mask_row):
    rows, tok, chan = pair_rep.shape
    heads = w_t.shape[0]
    half = heads // 2
    vm = pl.BlockSpec(memory_space=pltpu.VMEM)
    return pl.pallas_call(
        bias_kernel,
        out_shape=[
            jax.ShapeDtypeStruct((half, rows, tok), BF16),
            jax.ShapeDtypeStruct((half, rows, tok), BF16),
            jax.ShapeDtypeStruct((rows, tok), F32),
            jax.ShapeDtypeStruct((rows, tok), F32),
            jax.ShapeDtypeStruct((heads, rows, tok), F32),
        ],
        in_specs=[pl.BlockSpec(memory_space=pltpu.SMEM)] + [vm] * 4,
        out_specs=[vm] * 5,
        compiler_params=pltpu.CompilerParams(vmem_limit_bytes=VMEM_LIMIT),
        cost_estimate=pl.CostEstimate(flops=int(3e9), bytes_accessed=int(4e6), transcendentals=0),
        name="pair_bias",
    )(core, pair_rep, gain, w_t, mask_row)


def project_kernel(core_ref, act_ref, cot_ref, wq_ref, wk_ref, wv_ref, wo_ref, mask_ref, q_ref, k_ref, v_ref, d_ref):
    act = act_ref[0]
    for weight, out in ((wq_ref, q_ref), (wk_ref, k_ref), (wv_ref, v_ref)):
        out[0] = dot(act, weight[...]).T.astype(BF16)
    live = mask_ref[...] > 0
    d_ref[0] = jnp.where(live, dot(wo_ref[...], cot_ref[0], NT), 0.0).astype(BF16)


def project_call(core, act, cot, w_query, w_key, w_value, w_out, mask_row):
    samples, tok, width = act.shape
    half = width // 2
    columns = pl.BlockSpec((width, half), lambda s, c: (0, c[0]))
    per_sample = pl.BlockSpec((1, tok, width), lambda s, c: (s, 0, 0))
    out = pl.BlockSpec((1, half, tok), lambda s, c: (s, 0, 0))
    return pl.pallas_call(
        project_kernel,
        grid_spec=pltpu.PrefetchScalarGridSpec(
            num_scalar_prefetch=1,
            grid=(samples,),
            in_specs=[per_sample, per_sample, columns, columns, columns,
                      pl.BlockSpec((half, width), lambda s, c: (c[0], 0)),
                      pl.BlockSpec((1, tok), lambda s, c: (0, 0))],
            out_specs=[out] * 4,
        ),
        out_shape=[jax.ShapeDtypeStruct((samples, half, tok), BF16)] * 4,
        compiler_params=pltpu.CompilerParams(vmem_limit_bytes=VMEM_LIMIT),
        cost_estimate=pl.CostEstimate(
            flops=8 * samples * tok * width * half, bytes_accessed=int(6e6), transcendentals=0
        ),
        name="projections",
    )(core, act, cot, w_query, w_key, w_value, w_out, mask_row)


def code16(block):
    top = jnp.max(jnp.abs(block), axis=0, keepdims=True)
    level = jnp.ceil(jnp.log2(jnp.maximum(top, 1.2e-38)) * 64.0) + 1.0
    unit = block * jnp.exp2(level * (-1.0 / 64.0))
    return jnp.round(unit * 32766.0).astype(jnp.int32).astype(jnp.int16), level


def decode16(codes, levels):
    scale = jnp.exp2(levels * (1.0 / 64.0)) * (1.0 / 32766.0)
    return codes.astype(jnp.int32).astype(F32) * scale


def pack_levels(levels):
    block = jnp.concatenate(levels, axis=0)
    if block.shape[0] < 8:
        block = jnp.concatenate([block, jnp.zeros((8 - block.shape[0], block.shape[1]), F32)], axis=0)
    return jnp.concatenate([block, block], axis=0).astype(jnp.int32).astype(jnp.int16)


def attention_kernel(arrays, head_width, offs_ref, *refs):
    bias_refs = refs[:arrays]
    q0, k0, v0, d0, q1, k1, v1, d1 = refs[arrays : arrays + 8]
    mixed0, mixed1, own_ref, code_ref, bias_f, grad, held = refs[arrays + 8 :]
    stay, _, rows, _ = own_ref.shape
    part = rows // 2
    head, chunk = pl.program_id(0), pl.num_programs(0)
    at = 0
    for ref in bias_refs:
        for b in range(ref.shape[0]):
            block = ref[b, 0].astype(F32) * LOG2E
            for side in range(2):
                start = pl.multiple_of(offs_ref[at], 8)
                bias_f[pl.ds(start, part), :] = block[side * part : (side + 1) * part]
                at += 1
    factor = head_width ** (-0.5) * LOG2E
    count = q0.shape[0]

    def products(s):
        qr, kr, vr, dr = (q0, k0, v0, d0) if s < count else (q1, k1, v1, d1)
        at = s % count
        return dot(qr[at].T, kr[at]), dot(dr[at].T, vr[at]), vr[at].T

    total = None
    ahead = products(0)
    for s in range(2 * count):
        scores, d_probs, value = ahead
        if s + 1 < 2 * count:
            ahead = products(s + 1)
        scores = scores * factor + bias_f[...]
        exps = jnp.exp2(scores - jnp.max(scores, axis=1, keepdims=True))
        probs = exps * (1.0 / jnp.sum(exps, axis=1, keepdims=True))
        mixed = mixed0 if s < count else mixed1
        mixed[s % count] = dot(probs.astype(BF16), value).T.astype(BF16)
        delta = jnp.sum(probs * d_probs, axis=1, keepdims=True)
        d_scores = probs * (d_probs - delta)
        total = d_scores if total is None else total + d_scores
    grad[...] = total

    @pl.when(head == 0)
    def _():
        held[...] = jnp.zeros_like(held)

    for b in range(2 * stay):
        starts = [pl.multiple_of(offs_ref[4 * stay + 2 * b + side], 8) for side in range(2)]
        block = jnp.concatenate([grad[pl.ds(start, part), :] for start in starts], axis=0)
        if b < stay:
            own_ref[b, 0] = block
        else:
            codes, level = code16(block)
            code_ref[b - stay, pl.ds(pl.multiple_of(head * rows, 16), rows), :] = codes
            held[b - stay, pl.ds(head, 1), :] = level

    @pl.when(head == chunk - 1)
    def _():
        last = code_ref.shape[1] - 16
        for b in range(stay):
            code_ref[b, last:, :] = pack_levels([held[b]])


def attention_call(head_width, offsets, bias_arrays, first, own_proj, sib_proj):
    blocks = sum(array.shape[0] for array in bias_arrays)
    _, chunk, rows, tok = bias_arrays[0].shape
    count = own_proj[0].shape[0]
    stay = blocks // 2
    head = pl.BlockSpec((count, head_width, tok), lambda h, o: (0, first + h, 0))
    mixed = pl.BlockSpec((count, head_width, tok), lambda h, o: (0, h, 0))
    coded = (stay, chunk * rows + 16, tok)
    tiles = 2 * count * chunk
    return pl.pallas_call(
        functools.partial(attention_kernel, len(bias_arrays), head_width),
        grid_spec=pltpu.PrefetchScalarGridSpec(
            num_scalar_prefetch=1,
            grid=(chunk,),
            in_specs=[
                pl.BlockSpec((array.shape[0], 1, rows, tok), lambda h, o: (0, h, 0, 0)) for array in bias_arrays
            ]
            + [head] * 8,
            out_specs=[
                mixed,
                mixed,
                pl.BlockSpec((stay, 1, rows, tok), lambda h, o: (0, h, 0, 0)),
                pl.BlockSpec(coded, lambda h, o: (0, 0, 0)),
            ],
            scratch_shapes=[
                pltpu.VMEM((tok, tok), F32),
                pltpu.VMEM((tok, tok), F32),
                pltpu.VMEM((stay, 8, tok), F32),
            ],
        ),
        out_shape=[
            jax.ShapeDtypeStruct((count, chunk * head_width, tok), BF16),
            jax.ShapeDtypeStruct((count, chunk * head_width, tok), BF16),
            jax.ShapeDtypeStruct((stay, chunk, rows, tok), F32),
            jax.ShapeDtypeStruct(coded, jnp.int16),
        ],
        compiler_params=pltpu.CompilerParams(vmem_limit_bytes=VMEM_LIMIT),
        cost_estimate=pl.CostEstimate(
            flops=tiles * 6 * tok * tok * 256, bytes_accessed=int(4e6), transcendentals=tiles * tok * tok
        ),
        name="attention",
    )(offsets, *bias_arrays, *own_proj, *sib_proj)


def plain_call(kernel, name, out_shape, *operands):
    vm = pl.BlockSpec(memory_space=pltpu.VMEM)
    return pl.pallas_call(
        kernel,
        in_specs=[vm] * len(operands),
        out_specs=[vm] * len(out_shape),
        out_shape=out_shape,
        compiler_params=pltpu.CompilerParams(vmem_limit_bytes=VMEM_LIMIT),
        cost_estimate=pl.CostEstimate(flops=int(4e6), bytes_accessed=int(3e6), transcendentals=0),
        name=name,
    )(*operands)


def join_kernel(own_ref, code_ref, stay_ref, next_ref):
    blocks, chunk, rows, _ = own_ref.shape
    last = chunk * rows
    stay = blocks // 2
    for b in range(blocks):
        levels = code_ref[b, last:, :].astype(jnp.int32).astype(F32)
        held = []
        for h in range(chunk):
            span = slice(h * rows, (h + 1) * rows)
            block = own_ref[b, h] + decode16(code_ref[b, span, :], levels[h : h + 1])
            if b < stay:
                stay_ref[b, h] = block
            else:
                codes, level = code16(block)
                next_ref[b - stay, span, :] = codes
                held.append(level)
        if held:
            next_ref[b - stay, last:, :] = pack_levels(held)


def join_call(own, codes):
    blocks, chunk, rows, tok = own.shape
    return plain_call(
        join_kernel,
        "join",
        [
            jax.ShapeDtypeStruct((blocks // 2, chunk, rows, tok), F32),
            jax.ShapeDtypeStruct((blocks // 2, chunk * rows + 16, tok), jnp.int16),
        ],
        own, codes,
    )


def total_kernel(own_ref, code_ref, here_ref, there_ref):
    _, chunk, rows, _ = own_ref.shape
    part = rows // 2
    levels = code_ref[0, chunk * rows :, :].astype(jnp.int32).astype(F32)
    for h in range(chunk):
        block = own_ref[0, h] + decode16(code_ref[0, h * rows : (h + 1) * rows, :], levels[h : h + 1])
        here_ref[h] = block[:part]
        there_ref[h] = block[part:]


def total_call(own, codes):
    _, chunk, rows, tok = own.shape
    return plain_call(
        total_kernel, "last_join", [jax.ShapeDtypeStruct((chunk, rows // 2, tok), F32)] * 2, own, codes
    )


def output_kernel(parts, core_ref, *refs):
    own_refs, other_refs = refs[:parts], refs[parts : 2 * parts]
    w_own, w_other, mask_ref, out_ref = refs[2 * parts :]
    live = mask_ref[...] > 0
    total = None
    for group, weight in ((own_refs, w_own), (other_refs, w_other)):
        start = 0
        for ref in group:
            size = ref.shape[1]
            mixed = ref[0]
            mixed = jnp.where(live, mixed.astype(F32), 0.0).T.astype(BF16)
            term = dot(mixed, weight[start : start + size, :])
            total = term if total is None else total + term
            start += size
    out_ref[0] = total.astype(BF16)


def output_call(core, own, other, w_out, mask_row):
    samples, size, tok = own[0].shape
    parts = len(own)
    width = w_out.shape[0]
    half = width // 2
    block = pl.BlockSpec((1, size, tok), lambda s, c: (s, 0, 0))
    return pl.pallas_call(
        functools.partial(output_kernel, parts),
        grid_spec=pltpu.PrefetchScalarGridSpec(
            num_scalar_prefetch=1,
            grid=(samples,),
            in_specs=[block] * (2 * parts)
            + [
                pl.BlockSpec((half, width), lambda s, c: (c[0], 0)),
                pl.BlockSpec((half, width), lambda s, c: (1 - c[0], 0)),
                pl.BlockSpec((1, tok), lambda s, c: (0, 0)),
            ],
            out_specs=pl.BlockSpec((1, tok, width), lambda s, c: (s, 0, 0)),
        ),
        out_shape=jax.ShapeDtypeStruct((samples, tok, width), BF16),
        compiler_params=pltpu.CompilerParams(vmem_limit_bytes=VMEM_LIMIT),
        cost_estimate=pl.CostEstimate(
            flops=2 * samples * tok * width * width, bytes_accessed=int(4e6), transcendentals=0
        ),
        name="output",
    )(core, *own, *other, w_out, w_out, mask_row)


def load_rows(refs, i):
    return jnp.concatenate([ref[:, i, :] for ref in refs], axis=0)


def projection_kernel(parts, core_ref, *refs):
    own_refs, other_refs = refs[:parts], refs[parts : 2 * parts]
    pair_ref, gain_ref, mean_ref, rstd_ref, out_ref = refs[2 * parts :]
    rows, tok, chan = pair_ref.shape
    heads = out_ref.shape[0]
    half = heads // 2
    total = jnp.zeros((3 * heads, chan), F32)
    means = jnp.zeros((heads, tok), F32)
    for i in range(rows):
        grads = load_rows([*own_refs, *other_refs], i) * rstd_ref[i : i + 1, :]
        means = means + grads * mean_ref[i : i + 1, :]
        total = total + dot(jnp.concatenate(pieces3(grads), axis=0), pair_ref[i])
    raw = total[:heads] + (total[heads : 2 * heads] + total[2 * heads :])
    result = (raw - jnp.sum(means, axis=1, keepdims=True)) * gain_ref[...]
    core = core_ref[0]
    out_ref[pl.ds(pl.multiple_of(core * half, half), half), :] = result[:half]
    out_ref[pl.ds(pl.multiple_of((1 - core) * half, half), half), :] = result[half:]


def pair_grad_kernel(parts, core_ref, *refs):
    own_refs, other_refs = refs[:parts], refs[parts : 2 * parts]
    pair_ref, gain_ref, wt_ref, mean_ref, rstd_ref, bias_ref, out_ref = refs[2 * parts :]
    rows, tok, chan = pair_ref.shape
    half = wt_ref.shape[0] // 2
    core = core_ref[0]

    def own_first(take):
        return jnp.concatenate([take(core * half), take((1 - core) * half)], axis=0)

    scaled = own_first(lambda at: wt_ref[pl.ds(pl.multiple_of(at, half), half), :]) * gain_ref[...]
    scaled = scaled - jnp.mean(scaled, axis=1, keepdims=True)
    wh, wm, wl = pieces3(scaled)
    project = jnp.concatenate([wh, wm, wh, wl, wm, wh], axis=0)
    count = project.shape[0]
    zero, one = jnp.zeros((8, chan), BF16), jnp.ones((8, chan), BF16)
    right = jnp.concatenate(
        [
            jnp.concatenate([project, jnp.zeros_like(project)], axis=1),
            jnp.concatenate([one, zero], axis=1),
            jnp.concatenate([zero, one], axis=1),
        ],
        axis=0,
    )
    fill = jnp.zeros((5, tok), F32)
    for i in range(rows):
        rstd = rstd_ref[i : i + 1, :]
        grads = load_rows([*own_refs, *other_refs], i) * rstd
        bias = own_first(lambda at: bias_ref[pl.ds(at, half), i, :])
        along = jnp.sum(grads * bias, axis=0, keepdims=True) * rstd * (1.0 / chan)
        gh, gm, gl = pieces3(grads)
        back = [piece.astype(F32) for piece in pieces3(along * mean_ref[i : i + 1, :])]
        slope = [piece.astype(F32) for piece in pieces3(along)]
        extra = jnp.concatenate([*back, fill, *slope, fill], axis=0).astype(BF16)
        left = jnp.concatenate([gh, gh, gm, gh, gm, gl, extra], axis=0)
        both = dot(left, right, TN)
        out_ref[i] = (both[:, :chan] - pair_ref[i].astype(F32) * both[:, chan:]).astype(BF16)


def final_call(kernel, name, core, own, other, operands, out_shape):
    vm = pl.BlockSpec(memory_space=pltpu.VMEM)
    parts = len(own)
    return pl.pallas_call(
        functools.partial(kernel, parts),
        in_specs=[pl.BlockSpec(memory_space=pltpu.SMEM)] + [vm] * (2 * parts + len(operands)),
        out_specs=vm,
        out_shape=out_shape,
        compiler_params=pltpu.CompilerParams(vmem_limit_bytes=VMEM_LIMIT),
        cost_estimate=pl.CostEstimate(flops=int(4e9), bytes_accessed=int(8e6), transcendentals=0),
        name=name,
    )(core, *own, *other, *operands)


def per_device_tiled(
    chips, activations, cotangent, pair_rep, pair_gain, w_pair, w_query, w_key, w_value, w_out, token_mask
):
    rows, tok, chan = pair_rep.shape
    heads = w_pair.shape[1]
    half = heads // 2
    head_width = w_query.shape[0] // heads
    core = lax.axis_index("core")
    chip = lax.axis_index("chip")
    bits = [1 << b for b in reversed(range(chips.bit_length() - 1))]

    def swap_core(x):
        return lax.ppermute(x, "core", [(0, 1), (1, 0)])

    def swap(x, bit):
        return lax.ppermute(x, "chip", [(c, c ^ bit) for c in range(chips)])

    masks = [0]
    for bit in bits:
        masks = masks + [m ^ bit for m in masks]
    places = [jnp.stack([chip ^ m for m in masks]), jnp.stack([chip * 0 + c for c in range(chips)])]
    sides = jnp.stack([core, 1 - core])

    def offsets_of(places_in):
        both = jnp.concatenate([places_in, places[0]])
        return (both[:, None] * (2 * rows) + sides[None, :] * rows).reshape(-1).astype(jnp.int32)

    doubled, gathered = [offsets_of(p) for p in places]
    core_1 = core.reshape(1).astype(jnp.int32)
    gain = pair_gain.reshape(1, chan)
    w_t = w_pair.T.astype(F32)
    mask_row = token_mask.reshape(1, tok)

    sib_act, sib_cot = swap_core(activations), swap_core(cotangent)
    bias_own, bias_other, mean_rows, rstd_rows, bias_rows = bias_call(core_1, pair_rep, gain, w_t, mask_row)
    bias_chip = jnp.concatenate([bias_own, swap_core(bias_other)], axis=1)[None]

    weights = (w_query, w_key, w_value, w_out)
    own_proj = project_call(core_1, activations, cotangent, *weights, mask_row)
    sib_proj = project_call(core_1, sib_act, sib_cot, *weights, mask_row)

    mixed_own, mixed_other, grads_own, grads_other = [], [], [], []
    first = 0
    for size, by_permute in CHUNKS:
        mine = bias_chip[:, first : first + size]
        if by_permute:
            for bit in bits[:-1]:
                mine = jnp.concatenate([mine, swap(mine, bit)], axis=0)
            arrays, offsets = [mine, swap(mine, bits[-1])], doubled
        else:
            arrays, offsets = [lax.all_gather(mine, "chip", axis=0, tiled=True)], gathered
        mixed0, mixed1, stay, codes = attention_call(head_width, offsets, arrays, first, own_proj, sib_proj)
        mixed_own.append(mixed0)
        mixed_other.append(swap_core(mixed1))
        for bit in reversed(bits[1:]):
            stay, codes = join_call(stay, swap(codes, bit))
        here, there = total_call(stay, swap(codes, bits[0]))
        grads_own.append(here)
        grads_other.append(swap_core(there))
        first += size

    attended = output_call(core_1, mixed_own, mixed_other, w_out, mask_row)
    projection = final_call(
        projection_kernel, "pair_projection", core_1, grads_own, grads_other,
        (pair_rep, gain, mean_rows, rstd_rows), jax.ShapeDtypeStruct((heads, chan), F32),
    )
    projection = projection + swap_core(projection)
    for bit in reversed(bits):
        projection = projection + swap(projection, bit)
    grad_pair = final_call(
        pair_grad_kernel, "pair_gradient", core_1, grads_own, grads_other,
        (pair_rep, gain, w_t, mean_rows, rstd_rows, bias_rows), jax.ShapeDtypeStruct(pair_rep.shape, BF16),
    )
    return (attended, grad_pair, projection.T)


def solution(mesh):
    split = P(("grp", "smp"), None, None)
    devices = mesh.shape["smp"]

    def run(activations, cotangent, pair_rep, pair_gain, w_pair, *rest):
        parts = mesh.shape["grp"]
        rows, heads, tok = pair_rep.shape[0] // (parts * devices), w_pair.shape[1], pair_rep.shape[1]
        power = devices >= 8 and devices & (devices - 1) == 0
        if power and rows % 8 == 0 and rows <= 128 and heads == 2 * sum(size for size, _ in CHUNKS) and tok % 128 == 0:
            inner = Mesh(mesh.devices.reshape(parts, devices // 2, 2), ("grp", "chip", "core"))
            whole = P(("grp", "chip", "core"), None, None)
            body = functools.partial(per_device_tiled, devices // 2)
        else:
            inner, whole, body = mesh, split, per_device_plain
        return jax.shard_map(
            body,
            mesh=inner,
            in_specs=(whole, whole, whole, P(), P(), P(), P(), P(), P(), P("grp")),
            out_specs=(whole, whole, P("grp", None)),
            check_vma=False,
        )(activations, cotangent, pair_rep, pair_gain, w_pair, *rest)

    return run
```

```python
import functools
import math

import jax
import jax.numpy as jnp
from jax import lax
from jax.experimental import pallas as pl
from jax.experimental.pallas import tpu as pltpu
from jax.sharding import Mesh
from jax.sharding import PartitionSpec as P

F32 = jnp.float32
BF16 = jnp.bfloat16
LOG2E = math.log2(math.e)
NT = (((1,), (1,)), ((), ()))
TN = (((0,), (0,)), ((), ()))
COST = pl.CostEstimate(flops=1000, bytes_accessed=1000, transcendentals=0)
VMEM_LIMIT = 48 * 1024 * 1024
VMEM_WIDE = 60 * 1024 * 1024
CHUNKS = (3, 3, 2)
GATHER_OTHER = (2,)
SCATTER_OTHER = (0,)
EARLY = 9
LATE = False


def normalize(pair_rep, pair_gain):
    values_f = pair_rep.astype(F32)
    centre = jnp.mean(values_f, axis=-1, keepdims=True)
    spread = jnp.mean((values_f - centre) ** 2, axis=-1, keepdims=True)
    rstd = lax.rsqrt(spread + 1e-05)
    centred = (values_f - centre) * rstd
    return (centred * pair_gain, centred, rstd)


def per_device_plain(
    activations, cotangent, pair_rep, pair_gain, w_pair, w_query, w_key, w_value, w_out, token_mask
):
    head_count = w_pair.shape[1]
    model_width = w_query.shape[0]
    head_width = model_width // head_count
    tok_count = token_mask.shape[0]
    normed, centred, rstd = normalize(pair_rep, pair_gain)
    bias_rows = jnp.einsum(
        "rjc,ch->rhj", normed, w_pair.astype(F32), precision=lax.Precision.HIGHEST
    ).astype(BF16)
    bias_full = lax.all_gather(bias_rows, "smp", axis=0, tiled=True).astype(F32)
    live_keys = token_mask > 0
    outputs = []
    grad_total = None
    for sample_index in range(activations.shape[0]):
        sample_act = activations[sample_index]

        def project(weight):
            return (
                jnp.dot(sample_act, weight, preferred_element_type=F32)
                .astype(BF16)
                .reshape(tok_count, head_count, head_width)
            )

        queries, keys_proj, values_proj = project(w_query), project(w_key), project(w_value)
        scores = (
            jnp.einsum("ihd,jhd->ihj", queries, keys_proj, preferred_element_type=F32)
            * head_width ** (-0.5)
            + bias_full
        )
        scores = jnp.where(live_keys[None, None, :], scores, -1e30)
        exps = jnp.exp(scores - jnp.max(scores, axis=-1, keepdims=True))
        probs = exps / jnp.sum(exps, axis=-1, keepdims=True)
        mixed = (
            jnp.einsum("ihj,jhd->ihd", probs.astype(BF16), values_proj, preferred_element_type=F32)
            .astype(BF16)
            .reshape(tok_count, model_width)
        )
        output = jnp.dot(mixed, w_out, preferred_element_type=F32)
        outputs.append(jnp.where(live_keys[:, None], output, 0.0).astype(BF16))
        sample_cot = cotangent[sample_index]
        masked_cot = jnp.where(live_keys[:, None], sample_cot, jnp.zeros_like(sample_cot))
        d_mixed = (
            jnp.dot(masked_cot, w_out.T, preferred_element_type=F32)
            .astype(BF16)
            .reshape(tok_count, head_count, head_width)
        )
        d_probs = jnp.einsum("ihd,jhd->ihj", d_mixed, values_proj, preferred_element_type=F32)
        d_scores = probs * (d_probs - jnp.sum(probs * d_probs, axis=-1, keepdims=True))
        grad_total = d_scores if grad_total is None else grad_total + d_scores
    bias_grad = lax.psum_scatter(grad_total, "smp", scatter_dimension=0, tiled=True)
    proj_local = jnp.einsum("rjc,rhj->ch", normed, bias_grad, precision=lax.Precision.HIGHEST)
    grad_projection = lax.psum(proj_local, "smp")
    d_normed = (
        jnp.einsum("rhj,ch->rjc", bias_grad, w_pair.astype(F32), precision=lax.Precision.HIGHEST)
        * pair_gain
    )
    first_mean = jnp.mean(d_normed, axis=-1, keepdims=True)
    second_mean = jnp.mean(d_normed * centred, axis=-1, keepdims=True)
    grad_pair = (rstd * (d_normed - first_mean - centred * second_mean)).astype(BF16)
    return (jnp.stack(outputs), grad_pair, grad_projection)


def dot(left, right, dims=None):
    if dims is None:
        return jnp.dot(left, right, preferred_element_type=F32)
    return lax.dot_general(left, right, dims, preferred_element_type=F32)


def pieces3(value):
    high = value.astype(BF16)
    rest = value - high.astype(F32)
    mid = rest.astype(BF16)
    low = (rest - mid.astype(F32)).astype(BF16)
    return high, mid, low


def bias_kernel(core_ref, pair_ref, gain_ref, wt_ref, mask_ref, own_ref, other_ref, mean_ref, rstd_ref, held):
    rows, tok, chan = pair_ref.shape
    heads = wt_ref.shape[1]
    half = heads // 2
    scaled = wt_ref[...].astype(F32).T * gain_ref[...]
    total = jnp.sum(scaled, axis=1, keepdims=True)
    left = jnp.concatenate([*pieces3(scaled), jnp.ones((16, chan), BF16)], axis=0)
    lane = lax.broadcasted_iota(jnp.int32, (tok, 128), 1)
    spreads = jnp.zeros((tok, 128), F32)
    for i in range(rows):
        values = pair_ref[i].astype(F32)
        diff = values - jnp.sum(values, axis=1, keepdims=True) * (1.0 / chan)
        spread = jnp.sum(diff * diff, axis=1, keepdims=True) * (1.0 / chan)
        spreads = jnp.where(lane == i, spread, spreads)
    rstd = lax.rsqrt(spreads.T[:rows] + 1e-05)
    rstd_ref[...] = rstd
    for i in range(rows):
        sums = dot(left, pair_ref[i], NT)
        mean_row = sums[3 * heads : 3 * heads + 1] * (1.0 / chan)
        raw = sums[0:heads] + (sums[heads : 2 * heads] + sums[2 * heads : 3 * heads])
        held[:, i, :] = (raw - total * mean_row) * rstd[i : i + 1]
        mean_ref[i : i + 1, :] = mean_row
    core = core_ref[0]
    live = (mask_ref[...].reshape(1, 1, tok) > 0)
    own_ref[...] = jnp.where(live, held[pl.ds(core * half, half)], -1e30).astype(BF16)
    other_ref[...] = jnp.where(live, held[pl.ds((1 - core) * half, half)], -1e30).astype(BF16)


def bias_call(core, pair_rep, gain, w_pair, mask_row):
    rows, tok, chan = pair_rep.shape
    heads = w_pair.shape[1]
    half = heads // 2
    vm = pl.BlockSpec(memory_space=pltpu.VMEM)
    return pl.pallas_call(
        bias_kernel,
        out_shape=[
            jax.ShapeDtypeStruct((half, rows, tok), BF16),
            jax.ShapeDtypeStruct((half, rows, tok), BF16),
            jax.ShapeDtypeStruct((rows, tok), F32),
            jax.ShapeDtypeStruct((rows, tok), F32),
            jax.ShapeDtypeStruct((heads, rows, tok), F32),
        ],
        in_specs=[pl.BlockSpec(memory_space=pltpu.SMEM)] + [vm] * 4,
        out_specs=[vm] * 5,
        compiler_params=pltpu.CompilerParams(vmem_limit_bytes=VMEM_LIMIT),
        cost_estimate=COST,
        name="pair_bias",
    )(core, pair_rep, gain, w_pair, mask_row)


def project_kernel(core_ref, act_ref, cot_ref, wq_ref, wk_ref, wv_ref, wo_ref, mask_ref, q_ref, k_ref, v_ref, d_ref):
    act = act_ref[0]
    for weight, out in ((wq_ref, q_ref), (wk_ref, k_ref), (wv_ref, v_ref)):
        out[0] = dot(act, weight[...]).T.astype(BF16)
    live = mask_ref[...] > 0
    d_ref[0] = jnp.where(live, dot(wo_ref[...], cot_ref[0], NT), 0.0).astype(BF16)


def project_call(core, act, cot, w_query, w_key, w_value, w_out, mask_row):
    samples, tok, width = act.shape
    half = width // 2
    columns = pl.BlockSpec((width, half), lambda s, c: (0, c[0]))
    per_sample = pl.BlockSpec((1, tok, width), lambda s, c: (s, 0, 0))
    out = pl.BlockSpec((1, half, tok), lambda s, c: (s, 0, 0))
    return pl.pallas_call(
        project_kernel,
        grid_spec=pltpu.PrefetchScalarGridSpec(
            num_scalar_prefetch=1,
            grid=(samples,),
            in_specs=[per_sample, per_sample, columns, columns, columns,
                      pl.BlockSpec((half, width), lambda s, c: (c[0], 0)),
                      pl.BlockSpec((1, tok), lambda s, c: (0, 0))],
            out_specs=[out] * 4,
        ),
        out_shape=[jax.ShapeDtypeStruct((samples, half, tok), BF16)] * 4,
        compiler_params=pltpu.CompilerParams(vmem_limit_bytes=VMEM_WIDE),
        cost_estimate=COST,
        name="projections",
    )(core, act, cot, w_query, w_key, w_value, w_out, mask_row)


def code16(block):
    top = jnp.max(jnp.abs(block), axis=0, keepdims=True)
    level = jnp.ceil(jnp.log2(jnp.maximum(top, 1.2e-38)) * 64.0) + 1.0
    unit = block * jnp.exp2(level * (-1.0 / 64.0))
    return jnp.round(unit * 32766.0).astype(jnp.int32).astype(jnp.int16), level


def decode16(codes, levels):
    scale = jnp.exp2(levels * (1.0 / 64.0)) * (1.0 / 32766.0)
    return codes.astype(jnp.int32).astype(F32) * scale


def pack_levels(levels):
    block = jnp.concatenate(levels, axis=0)
    if block.shape[0] < 8:
        block = jnp.concatenate([block, jnp.zeros((8 - block.shape[0], block.shape[1]), F32)], axis=0)
    return jnp.concatenate([block, block], axis=0).astype(jnp.int32).astype(jnp.int16)


def attention_kernel(arrays, head_width, masks, out_masks, place_ref, *refs):
    bias_refs = refs[:arrays]
    q0, k0, v0, d0, q1, k1, v1, d1 = refs[arrays : arrays + 8]
    mixed0, mixed1, own_ref, code_ref, bias_f, grad, held = refs[arrays + 8 :]
    stay, _, rows, _ = own_ref.shape
    part = rows // 2
    head, chunk = pl.program_id(0), pl.num_programs(0)
    chip, core = place_ref[0], place_ref[1]

    def starts(mask):
        first = (chip ^ mask) * rows
        return [pl.multiple_of(first + side * part, 8) for side in (core, 1 - core)]

    blocks = [(ref, b) for ref in bias_refs for b in range(ref.shape[0])]
    for mask, (ref, b) in zip(masks, blocks):
        block = ref[b, 0].astype(F32) * LOG2E
        for side, start in enumerate(starts(mask)):
            bias_f[pl.ds(start, part), :] = block[side * part : (side + 1) * part]
    factor = head_width ** (-0.5) * LOG2E
    count = q0.shape[0]

    def products(s):
        qr, kr, vr, dr = (q0, k0, v0, d0) if s < count else (q1, k1, v1, d1)
        at = s % count
        return dot(qr[at].T, kr[at]), dot(dr[at].T, vr[at]), vr[at].T

    total = None
    ahead = products(0)
    for s in range(2 * count):
        scores, d_probs, value = ahead
        if s + 1 < 2 * count:
            ahead = products(s + 1)
        scores = scores * factor + bias_f[...]
        exps = jnp.exp2(scores - jnp.max(scores, axis=1, keepdims=True))
        probs = exps * (1.0 / jnp.sum(exps, axis=1, keepdims=True))
        mixed = mixed0 if s < count else mixed1
        mixed[s % count] = dot(probs.astype(BF16), value).T.astype(BF16)
        delta = jnp.sum(probs * d_probs, axis=1, keepdims=True)
        d_scores = probs * (d_probs - delta)
        total = d_scores if total is None else total + d_scores
    grad[...] = total

    @pl.when(head == 0)
    def _():
        held[...] = jnp.zeros_like(held)

    for b, mask in enumerate(out_masks):
        block = jnp.concatenate([grad[pl.ds(start, part), :] for start in starts(mask)], axis=0)
        if b < stay:
            own_ref[b, 0] = block
        else:
            codes, level = code16(block)
            code_ref[b - stay, pl.ds(pl.multiple_of(head * rows, 16), rows), :] = codes
            held[b - stay, pl.ds(head, 1), :] = level

    @pl.when(head == chunk - 1)
    def _():
        last = code_ref.shape[1] - 16
        for b in range(stay):
            code_ref[b, last:, :] = pack_levels([held[b]])


def attention_call(head_width, masks, out_masks, place, bias_arrays, first, own_proj, sib_proj):
    blocks = len(masks)
    _, chunk, rows, tok = bias_arrays[0].shape
    count = own_proj[0].shape[0]
    stay = blocks // 2
    head = pl.BlockSpec((count, head_width, tok), lambda h, _: (0, first + h, 0))
    mixed = pl.BlockSpec((count, head_width, tok), lambda h, o: (0, h, 0))
    coded = (stay, chunk * rows + 16, tok)
    tiles = 2 * count * chunk
    return pl.pallas_call(
        functools.partial(attention_kernel, len(bias_arrays), head_width, masks, out_masks),
        grid_spec=pltpu.PrefetchScalarGridSpec(
            num_scalar_prefetch=1,
            grid=(chunk,),
            in_specs=[
                pl.BlockSpec((array.shape[0], 1, rows, tok), lambda h, o: (0, h, 0, 0)) for array in bias_arrays
            ]
            + [head] * 8,
            out_specs=[
                mixed,
                mixed,
                pl.BlockSpec((stay, 1, rows, tok), lambda h, o: (0, h, 0, 0)),
                pl.BlockSpec(coded, lambda h, o: (0, 0, 0)),
            ],
            scratch_shapes=[
                pltpu.VMEM((tok, tok), F32),
                pltpu.VMEM((tok, tok), F32),
                pltpu.VMEM((stay, 8, tok), F32),
            ],
        ),
        out_shape=[
            jax.ShapeDtypeStruct((count, chunk * head_width, tok), BF16),
            jax.ShapeDtypeStruct((count, chunk * head_width, tok), BF16),
            jax.ShapeDtypeStruct((stay, chunk, rows, tok), F32),
            jax.ShapeDtypeStruct(coded, jnp.int16),
        ],
        compiler_params=pltpu.CompilerParams(vmem_limit_bytes=VMEM_WIDE),
        cost_estimate=COST,
        name="attention",
    )(place, *bias_arrays, *own_proj, *sib_proj)


def plain_call(kernel, name, out_shape, *operands):
    vm = pl.BlockSpec(memory_space=pltpu.VMEM)
    return pl.pallas_call(
        kernel,
        in_specs=[vm] * len(operands),
        out_specs=[vm] * len(out_shape),
        out_shape=out_shape,
        compiler_params=pltpu.CompilerParams(vmem_limit_bytes=VMEM_LIMIT),
        cost_estimate=COST,
        name=name,
    )(*operands)


def concat_kernel(*refs):
    out_ref, at = refs[-1], 0
    for ref in refs[:-1]:
        out_ref[at : at + ref.shape[0]] = ref[...]
        at += ref.shape[0]


def concat_call(*arrays):
    blocks = sum(x.shape[0] for x in arrays)
    return plain_call(concat_kernel, "concat", [jax.ShapeDtypeStruct((blocks, *arrays[0].shape[1:]), BF16)], *arrays)[0]


def join_kernel(own_ref, code_ref, stay_ref, next_ref):
    blocks, chunk, rows, _ = own_ref.shape
    last = chunk * rows
    stay = blocks // 2
    for b in range(blocks):
        levels = code_ref[b, last:, :].astype(jnp.int32).astype(F32)
        held = []
        for h in range(chunk):
            span = slice(h * rows, (h + 1) * rows)
            block = own_ref[b, h] + decode16(code_ref[b, span, :], levels[h : h + 1])
            if b < stay:
                stay_ref[b, h] = block
            else:
                codes, level = code16(block)
                next_ref[b - stay, span, :] = codes
                held.append(level)
        if held:
            next_ref[b - stay, last:, :] = pack_levels(held)


def join_call(own, codes):
    blocks, chunk, rows, tok = own.shape
    return plain_call(
        join_kernel,
        "join",
        [
            jax.ShapeDtypeStruct((blocks // 2, chunk, rows, tok), F32),
            jax.ShapeDtypeStruct((blocks // 2, chunk * rows + 16, tok), jnp.int16),
        ],
        own, codes,
    )


def total_kernel(own_ref, code_ref, here_ref, there_ref):
    _, chunk, rows, _ = own_ref.shape
    part = rows // 2
    levels = code_ref[0, chunk * rows :, :].astype(jnp.int32).astype(F32)
    for h in range(chunk):
        block = own_ref[0, h] + decode16(code_ref[0, h * rows : (h + 1) * rows, :], levels[h : h + 1])
        here_ref[h] = block[:part]
        there_ref[h] = block[part:]


def total_call(own, codes):
    _, chunk, rows, tok = own.shape
    return plain_call(
        total_kernel, "last_join", [jax.ShapeDtypeStruct((chunk, rows // 2, tok), F32)] * 2, own, codes
    )


def output_kernel(parts, core_ref, *refs):
    own_refs, other_refs = refs[:parts], refs[parts : 2 * parts]
    w_own, w_other, mask_ref, out_ref = refs[2 * parts :]
    live = mask_ref[...] > 0
    total = None
    for group, weight in ((own_refs, w_own), (other_refs, w_other)):
        start = 0
        for ref in group:
            size = ref.shape[1]
            mixed = ref[0]
            mixed = jnp.where(live, mixed.astype(F32), 0.0).T.astype(BF16)
            term = dot(mixed, weight[start : start + size, :])
            total = term if total is None else total + term
            start += size
    out_ref[0] = total.astype(BF16)


def output_call(core, own, other, w_out, mask_row):
    samples, _, tok = own[0].shape
    parts = len(own)
    width = w_out.shape[0]
    half = width // 2
    blocks = [pl.BlockSpec((1, x.shape[1], tok), lambda s, c: (s, 0, 0)) for x in (*own, *other)]
    return pl.pallas_call(
        functools.partial(output_kernel, parts),
        grid_spec=pltpu.PrefetchScalarGridSpec(
            num_scalar_prefetch=1,
            grid=(samples,),
            in_specs=blocks
            + [
                pl.BlockSpec((half, width), lambda s, c: (c[0], 0)),
                pl.BlockSpec((half, width), lambda s, c: (1 - c[0], 0)),
                pl.BlockSpec((1, tok), lambda s, c: (0, 0)),
            ],
            out_specs=pl.BlockSpec((1, tok, width), lambda s, c: (s, 0, 0)),
        ),
        out_shape=jax.ShapeDtypeStruct((samples, tok, width), BF16),
        compiler_params=pltpu.CompilerParams(vmem_limit_bytes=VMEM_WIDE),
        cost_estimate=COST,
        name="output",
    )(core, *own, *other, w_out, w_out, mask_row)


def load_rows(refs, i):
    return jnp.concatenate([ref[:, i, :] for ref in refs], axis=0)


def projection_kernel(parts, core_ref, *refs):
    own_refs, other_refs = refs[:parts], refs[parts : 2 * parts]
    pair_ref, gain_ref, mean_ref, rstd_ref, out_ref = refs[2 * parts :]
    rows, tok, chan = pair_ref.shape
    heads = out_ref.shape[0]
    half = heads // 2
    total = jnp.zeros((3 * heads, chan), F32)
    means = jnp.zeros((heads, tok), F32)
    for i in range(rows):
        grads = load_rows([*own_refs, *other_refs], i) * rstd_ref[i : i + 1, :]
        means = means + grads * mean_ref[i : i + 1, :]
        total = total + dot(jnp.concatenate(pieces3(grads), axis=0), pair_ref[i])
    raw = total[:heads] + (total[heads : 2 * heads] + total[2 * heads :])
    result = (raw - jnp.sum(means, axis=1, keepdims=True)) * gain_ref[...]
    core = core_ref[0]
    out_ref[pl.ds(pl.multiple_of(core * half, half), half), :] = result[:half]
    out_ref[pl.ds(pl.multiple_of((1 - core) * half, half), half), :] = result[half:]


def pair_grad_kernel(parts, core_ref, *refs):
    own_refs, other_refs = refs[:parts], refs[parts : 2 * parts]
    pair_ref, gain_ref, wt_ref, mean_ref, rstd_ref, bias_ref, out_ref, turned = refs[2 * parts :]
    rows, tok, chan = pair_ref.shape
    half = wt_ref.shape[1] // 2
    core = core_ref[0]
    turned[...] = wt_ref[...].astype(F32).T

    def own_first(take):
        return jnp.concatenate([take(core * half), take((1 - core) * half)], axis=0)

    scaled = own_first(lambda at: turned[pl.ds(pl.multiple_of(at, half), half), :]) * gain_ref[...]
    scaled = scaled - jnp.mean(scaled, axis=1, keepdims=True)
    wh, wm, wl = pieces3(scaled)
    project = jnp.concatenate([wh, wm, wh, wl, wm, wh], axis=0)
    count = project.shape[0]
    zero, one = jnp.zeros((8, chan), BF16), jnp.ones((8, chan), BF16)
    right = jnp.concatenate(
        [
            jnp.concatenate([project, jnp.zeros_like(project)], axis=1),
            jnp.concatenate([one, zero], axis=1),
            jnp.concatenate([zero, one], axis=1),
        ],
        axis=0,
    )
    fill = jnp.zeros((5, tok), F32)
    for i in range(rows):
        rstd = rstd_ref[i : i + 1, :]
        grads = load_rows([*own_refs, *other_refs], i) * rstd
        bias = own_first(lambda at: bias_ref[pl.ds(at, half), i, :])
        along = jnp.sum(grads * bias, axis=0, keepdims=True) * rstd * (1.0 / chan)
        gh, gm, gl = pieces3(grads)
        back = [piece.astype(F32) for piece in pieces3(along * mean_ref[i : i + 1, :])]
        slope = [piece.astype(F32) for piece in pieces3(along)]
        extra = jnp.concatenate([*back, fill, *slope, fill], axis=0).astype(BF16)
        left = jnp.concatenate([gh, gh, gm, gh, gm, gl, extra], axis=0)
        both = dot(left, right, TN)
        out_ref[i] = (both[:, :chan] - pair_ref[i].astype(F32) * both[:, chan:]).astype(BF16)


def final_call(kernel, name, core, own, other, operands, out_shape, scratch=()):
    vm = pl.BlockSpec(memory_space=pltpu.VMEM)
    parts = len(own)
    return pl.pallas_call(
        functools.partial(kernel, parts),
        in_specs=[pl.BlockSpec(memory_space=pltpu.SMEM)] + [vm] * (2 * parts + len(operands)),
        out_specs=vm,
        out_shape=out_shape,
        scratch_shapes=scratch,
        compiler_params=pltpu.CompilerParams(vmem_limit_bytes=VMEM_LIMIT),
        cost_estimate=COST,
        name=name,
    )(core, *own, *other, *operands)


def per_device_tiled(
    chips, activations, cotangent, pair_rep, pair_gain, w_pair, w_query, w_key, w_value, w_out, token_mask
):
    rows, tok, chan = pair_rep.shape
    heads = w_pair.shape[1]
    half = heads // 2
    head_width = w_query.shape[0] // heads
    core = lax.axis_index("core")
    chip = lax.axis_index("chip")
    bits = [1 << b for b in reversed(range(chips.bit_length() - 1))]

    def swap_core(x):
        return lax.ppermute(x, "core", [(0, 1), (1, 0)])

    def swap(x, bit):
        return lax.ppermute(x, "chip", [(c, c ^ bit) for c in range(chips)])

    tie = lax.optimization_barrier
    place = jnp.stack([chip, core]).astype(jnp.int32)
    core_1 = core.reshape(1).astype(jnp.int32)
    gain = pair_gain.reshape(1, chan)
    normal, other = bits, [*bits[:-2], bits[-1], bits[-2]]
    count, levels = len(CHUNKS), len(bits)
    gather_bits = [other if n in GATHER_OTHER else normal for n in range(count)]
    scatter_bits = [list(reversed(other if n in SCATTER_OTHER else normal)) for n in range(count)]

    def masks_of(order):
        masks = [0]
        for bit in order:
            masks = masks + [m ^ bit for m in masks]
        return masks

    sib_act, sib_cot = swap_core(activations), swap_core(cotangent)
    bias_own, bias_other, mean_rows, rstd_rows, bias_rows = bias_call(core_1, pair_rep, gain, w_pair, token_mask)
    bias_chip = jnp.concatenate([bias_own, swap_core(bias_other)], axis=1)[None]
    mask_row = token_mask.reshape(1, tok)
    weights = (w_query, w_key, w_value, w_out)
    own_proj = project_call(core_1, activations, cotangent, *weights, mask_row)
    sib_proj = project_call(core_1, sib_act, sib_cot, *weights, mask_row)

    firsts = [sum(CHUNKS[:n]) for n in range(count)]
    arrays = []
    for n, size in enumerate(CHUNKS):
        mine = bias_chip[:, firsts[n] : firsts[n] + size]
        for level, bit in enumerate(gather_bits[n][:-1]):
            coming = swap(mine, bit)
            if n == 0 and level == 0:
                coming, own_proj = tie((coming, own_proj))
            if n == 0 and level == 1:
                coming, sib_proj = tie((coming, sib_proj))
            mine = concat_call(mine, coming)
        arrays.append([mine, swap(mine, gather_bits[n][-1])])

    mixed_own, mixed_other, grads_own, grads_other = [], [], [], []
    far = [None] * count
    stays = [None] * count
    level_of = [0] * count

    def join(n):
        level_of[n] += 1
        stays[n], codes = join_call(stays[n], far[n])
        return codes

    for n in range(count):
        if n == count - 1 and n >= EARLY:
            for k in range(n - EARLY + 1):
                codes = join(k)
                codes, place = tie((codes, place))
                far[k] = swap(codes, scatter_bits[k][1])
        mixed0, mixed1, stays[n], codes = attention_call(
            head_width, masks_of(gather_bits[n]), masks_of(reversed(scatter_bits[n])),
            place, arrays[n], firsts[n], own_proj, sib_proj,
        )
        mixed_own.append(mixed0)
        mixed_other.append(mixed1)
        far[n] = swap(codes, scatter_bits[n][0])
    if LATE:
        first_join = join(1)
        first_join, *mixed_other = tie((first_join, *mixed_other))
        far[1] = swap(first_join, scatter_bits[1][1])
    mixed_other = [swap_core(mixed1) for mixed1 in mixed_other]
    attended = output_call(core_1, mixed_own, mixed_other, w_out, mask_row)
    for n in range(count):
        while level_of[n] < levels - 1:
            if n == count - 1 and level_of[n] == 1:
                far[n], attended = tie((far[n], attended))
            codes = join(n)
            far[n] = swap(codes, scatter_bits[n][level_of[n]])
        here, there = total_call(stays[n], far[n])
        grads_own.append(here)
        grads_other.append(swap_core(there))

    projection = final_call(
        projection_kernel, "pair_projection", core_1, grads_own, grads_other,
        (pair_rep, gain, mean_rows, rstd_rows), jax.ShapeDtypeStruct((heads, chan), F32),
    )
    rstd_rows, projection = tie((rstd_rows, projection))
    grad_pair = final_call(
        pair_grad_kernel, "pair_gradient", core_1, grads_own, grads_other,
        (pair_rep, gain, w_pair, mean_rows, rstd_rows, bias_rows), jax.ShapeDtypeStruct(pair_rep.shape, BF16),
        (pltpu.VMEM((heads, chan), F32),),
    )
    projection = projection + swap_core(projection)
    for bit in reversed(bits):
        other = swap(projection, bit)
        if bit == bits[-1]:
            other, grad_pair = tie((other, grad_pair))
        projection = projection + other
    return (attended, grad_pair, projection.T)


def solution(mesh):
    split = P(("grp", "smp"), None, None)
    devices = mesh.shape["smp"]

    def run(activations, cotangent, pair_rep, pair_gain, w_pair, *rest):
        parts = mesh.shape["grp"]
        rows, heads, tok = pair_rep.shape[0] // (parts * devices), w_pair.shape[1], pair_rep.shape[1]
        power = devices >= 8 and devices & (devices - 1) == 0
        if power and rows % 8 == 0 and rows <= 128 and heads == 2 * sum(CHUNKS) and tok % 128 == 0:
            inner = Mesh(mesh.devices.reshape(parts, devices // 2, 2), ("grp", "chip", "core"))
            whole = P(("grp", "chip", "core"), None, None)
            body = functools.partial(per_device_tiled, devices // 2)
        else:
            inner, whole, body = mesh, split, per_device_plain
        return jax.shard_map(
            body,
            mesh=inner,
            in_specs=(whole, whole, whole, P(), P(), P(), P(), P(), P(), P("grp")),
            out_specs=(whole, whole, P("grp", None)),
            check_vma=False,
        )(activations, cotangent, pair_rep, pair_gain, w_pair, *rest)

    return run
```

```python
import functools
import math

import jax
import jax.numpy as jnp
from jax import lax
from jax.experimental import pallas as pl
from jax.experimental.pallas import tpu as pltpu
from jax.sharding import Mesh
from jax.sharding import PartitionSpec as P

F32 = jnp.float32
BF16 = jnp.bfloat16
LOG2E = math.log2(math.e)
NT = (((1,), (1,)), ((), ()))
TN = (((0,), (0,)), ((), ()))
COST = pl.CostEstimate(flops=1000, bytes_accessed=1000, transcendentals=0)
VMEM_LIMIT = 48 * 1024 * 1024
VMEM_WIDE = 60 * 1024 * 1024
CHUNKS = (3, 3, 2)
GATHER_OTHER = ()
SCATTER_OTHER = (0,)
EARLY = 9
LATE = False


def normalize(pair_rep, pair_gain):
    values_f = pair_rep.astype(F32)
    centre = jnp.mean(values_f, axis=-1, keepdims=True)
    spread = jnp.mean((values_f - centre) ** 2, axis=-1, keepdims=True)
    rstd = lax.rsqrt(spread + 1e-05)
    centred = (values_f - centre) * rstd
    return (centred * pair_gain, centred, rstd)


def per_device_plain(
    activations, cotangent, pair_rep, pair_gain, w_pair, w_query, w_key, w_value, w_out, token_mask
):
    head_count = w_pair.shape[1]
    model_width = w_query.shape[0]
    head_width = model_width // head_count
    tok_count = token_mask.shape[0]
    normed, centred, rstd = normalize(pair_rep, pair_gain)
    bias_rows = jnp.einsum(
        "rjc,ch->rhj", normed, w_pair.astype(F32), precision=lax.Precision.HIGHEST
    ).astype(BF16)
    bias_full = lax.all_gather(bias_rows, "smp", axis=0, tiled=True).astype(F32)
    live_keys = token_mask > 0
    outputs = []
    grad_total = None
    for sample_index in range(activations.shape[0]):
        sample_act = activations[sample_index]

        def project(weight):
            return (
                jnp.dot(sample_act, weight, preferred_element_type=F32)
                .astype(BF16)
                .reshape(tok_count, head_count, head_width)
            )

        queries, keys_proj, values_proj = project(w_query), project(w_key), project(w_value)
        scores = (
            jnp.einsum("ihd,jhd->ihj", queries, keys_proj, preferred_element_type=F32)
            * head_width ** (-0.5)
            + bias_full
        )
        scores = jnp.where(live_keys[None, None, :], scores, -1e30)
        exps = jnp.exp(scores - jnp.max(scores, axis=-1, keepdims=True))
        probs = exps / jnp.sum(exps, axis=-1, keepdims=True)
        mixed = (
            jnp.einsum("ihj,jhd->ihd", probs.astype(BF16), values_proj, preferred_element_type=F32)
            .astype(BF16)
            .reshape(tok_count, model_width)
        )
        output = jnp.dot(mixed, w_out, preferred_element_type=F32)
        outputs.append(jnp.where(live_keys[:, None], output, 0.0).astype(BF16))
        sample_cot = cotangent[sample_index]
        masked_cot = jnp.where(live_keys[:, None], sample_cot, jnp.zeros_like(sample_cot))
        d_mixed = (
            jnp.dot(masked_cot, w_out.T, preferred_element_type=F32)
            .astype(BF16)
            .reshape(tok_count, head_count, head_width)
        )
        d_probs = jnp.einsum("ihd,jhd->ihj", d_mixed, values_proj, preferred_element_type=F32)
        d_scores = probs * (d_probs - jnp.sum(probs * d_probs, axis=-1, keepdims=True))
        grad_total = d_scores if grad_total is None else grad_total + d_scores
    bias_grad = lax.psum_scatter(grad_total, "smp", scatter_dimension=0, tiled=True)
    proj_local = jnp.einsum("rjc,rhj->ch", normed, bias_grad, precision=lax.Precision.HIGHEST)
    grad_projection = lax.psum(proj_local, "smp")
    d_normed = (
        jnp.einsum("rhj,ch->rjc", bias_grad, w_pair.astype(F32), precision=lax.Precision.HIGHEST)
        * pair_gain
    )
    first_mean = jnp.mean(d_normed, axis=-1, keepdims=True)
    second_mean = jnp.mean(d_normed * centred, axis=-1, keepdims=True)
    grad_pair = (rstd * (d_normed - first_mean - centred * second_mean)).astype(BF16)
    return (jnp.stack(outputs), grad_pair, grad_projection)


def dot(left, right, dims=None):
    if dims is None:
        return jnp.dot(left, right, preferred_element_type=F32)
    return lax.dot_general(left, right, dims, preferred_element_type=F32)


def pieces3(value):
    high = value.astype(BF16)
    rest = value - high.astype(F32)
    mid = rest.astype(BF16)
    low = (rest - mid.astype(F32)).astype(BF16)
    return high, mid, low


def bias_kernel(core_ref, pair_ref, gain_ref, wt_ref, mask_ref, own_ref, other_ref, mean_ref, rstd_ref, held):
    rows, tok, chan = pair_ref.shape
    heads = wt_ref.shape[1]
    half = heads // 2
    scaled = wt_ref[...].astype(F32).T * gain_ref[...]
    total = jnp.sum(scaled, axis=1, keepdims=True)
    left = jnp.concatenate([*pieces3(scaled), jnp.ones((16, chan), BF16)], axis=0)
    lane = lax.broadcasted_iota(jnp.int32, (tok, 128), 1)
    spreads = jnp.zeros((tok, 128), F32)
    for i in range(rows):
        values = pair_ref[i].astype(F32)
        diff = values - jnp.sum(values, axis=1, keepdims=True) * (1.0 / chan)
        spread = jnp.sum(diff * diff, axis=1, keepdims=True) * (1.0 / chan)
        spreads = jnp.where(lane == i, spread, spreads)
    rstd = lax.rsqrt(spreads.T[:rows] + 1e-05)
    rstd_ref[...] = rstd
    for i in range(rows):
        sums = dot(left, pair_ref[i], NT)
        mean_row = sums[3 * heads : 3 * heads + 1] * (1.0 / chan)
        raw = sums[0:heads] + (sums[heads : 2 * heads] + sums[2 * heads : 3 * heads])
        held[:, i, :] = (raw - total * mean_row) * rstd[i : i + 1]
        mean_ref[i : i + 1, :] = mean_row
    core = core_ref[0]
    live = (mask_ref[...].reshape(1, 1, tok) > 0)
    own_ref[...] = jnp.where(live, held[pl.ds(core * half, half)], -1e30).astype(BF16)
    other_ref[...] = jnp.where(live, held[pl.ds((1 - core) * half, half)], -1e30).astype(BF16)


def bias_call(core, pair_rep, gain, w_pair, mask_row):
    rows, tok, chan = pair_rep.shape
    heads = w_pair.shape[1]
    half = heads // 2
    vm = pl.BlockSpec(memory_space=pltpu.VMEM)
    return pl.pallas_call(
        bias_kernel,
        out_shape=[
            jax.ShapeDtypeStruct((half, rows, tok), BF16),
            jax.ShapeDtypeStruct((half, rows, tok), BF16),
            jax.ShapeDtypeStruct((rows, tok), F32),
            jax.ShapeDtypeStruct((rows, tok), F32),
            jax.ShapeDtypeStruct((heads, rows, tok), F32),
        ],
        in_specs=[pl.BlockSpec(memory_space=pltpu.SMEM)] + [vm] * 4,
        out_specs=[vm] * 5,
        compiler_params=pltpu.CompilerParams(vmem_limit_bytes=VMEM_LIMIT),
        cost_estimate=COST,
        name="pair_bias",
    )(core, pair_rep, gain, w_pair, mask_row)


def project_kernel(core_ref, act_ref, cot_ref, wq_ref, wk_ref, wv_ref, wo_ref, mask_ref, q_ref, k_ref, v_ref, d_ref):
    act = act_ref[0]
    for weight, out in ((wq_ref, q_ref), (wk_ref, k_ref), (wv_ref, v_ref)):
        out[0] = dot(act, weight[...]).T.astype(BF16)
    live = mask_ref[...] > 0
    d_ref[0] = jnp.where(live, dot(wo_ref[...], cot_ref[0], NT), 0.0).astype(BF16)


def project_call(core, act, cot, w_query, w_key, w_value, w_out, mask_row):
    samples, tok, width = act.shape
    half = width // 2
    columns = pl.BlockSpec((width, half), lambda s, c: (0, c[0]))
    per_sample = pl.BlockSpec((1, tok, width), lambda s, c: (s, 0, 0))
    out = pl.BlockSpec((1, half, tok), lambda s, c: (s, 0, 0))
    return pl.pallas_call(
        project_kernel,
        grid_spec=pltpu.PrefetchScalarGridSpec(
            num_scalar_prefetch=1,
            grid=(samples,),
            in_specs=[per_sample, per_sample, columns, columns, columns,
                      pl.BlockSpec((half, width), lambda s, c: (c[0], 0)),
                      pl.BlockSpec((1, tok), lambda s, c: (0, 0))],
            out_specs=[out] * 4,
        ),
        out_shape=[jax.ShapeDtypeStruct((samples, half, tok), BF16)] * 4,
        compiler_params=pltpu.CompilerParams(vmem_limit_bytes=VMEM_WIDE),
        cost_estimate=COST,
        name="projections",
    )(core, act, cot, w_query, w_key, w_value, w_out, mask_row)


def code16(block):
    top = jnp.max(jnp.abs(block), axis=0, keepdims=True)
    level = jnp.ceil(jnp.log2(jnp.maximum(top, 1.2e-38)) * 64.0) + 1.0
    unit = block * jnp.exp2(level * (-1.0 / 64.0))
    return jnp.round(unit * 32766.0).astype(jnp.int32).astype(jnp.int16), level


def decode16(codes, levels):
    scale = jnp.exp2(levels * (1.0 / 64.0)) * (1.0 / 32766.0)
    return codes.astype(jnp.int32).astype(F32) * scale


def pack_levels(levels):
    block = jnp.concatenate(levels, axis=0)
    if block.shape[0] < 8:
        block = jnp.concatenate([block, jnp.zeros((8 - block.shape[0], block.shape[1]), F32)], axis=0)
    return jnp.concatenate([block, block], axis=0).astype(jnp.int32).astype(jnp.int16)


def attention_kernel(arrays, head_width, masks, out_masks, place_ref, *refs):
    bias_refs = refs[:arrays]
    q0, k0, v0, d0, q1, k1, v1, d1 = refs[arrays : arrays + 8]
    mixed0, mixed1, own_ref, code_ref, bias_f, grad, held = refs[arrays + 8 :]
    stay, _, rows, _ = own_ref.shape
    part = rows // 2
    head, chunk = pl.program_id(0), pl.num_programs(0)
    chip, core = place_ref[0], place_ref[1]

    def starts(mask):
        first = (chip ^ mask) * rows
        return [pl.multiple_of(first + side * part, 8) for side in (core, 1 - core)]

    blocks = [(ref, b) for ref in bias_refs for b in range(ref.shape[0])]
    for mask, (ref, b) in zip(masks, blocks):
        block = ref[b, 0].astype(F32) * LOG2E
        for side, start in enumerate(starts(mask)):
            bias_f[pl.ds(start, part), :] = block[side * part : (side + 1) * part]
    factor = head_width ** (-0.5) * LOG2E
    count = q0.shape[0]

    def products(s):
        qr, kr, vr, dr = (q0, k0, v0, d0) if s < count else (q1, k1, v1, d1)
        at = s % count
        return dot(qr[at].T, kr[at]), dot(dr[at].T, vr[at]), vr[at].T

    total = None
    ahead = products(0)
    for s in range(2 * count):
        scores, d_probs, value = ahead
        if s + 1 < 2 * count:
            ahead = products(s + 1)
        scores = scores * factor + bias_f[...]
        exps = jnp.exp2(scores - jnp.max(scores, axis=1, keepdims=True))
        probs = exps * (1.0 / jnp.sum(exps, axis=1, keepdims=True))
        mixed = mixed0 if s < count else mixed1
        mixed[s % count] = dot(probs.astype(BF16), value).T.astype(BF16)
        delta = jnp.sum(probs * d_probs, axis=1, keepdims=True)
        d_scores = probs * (d_probs - delta)
        total = d_scores if total is None else total + d_scores
    grad[...] = total

    @pl.when(head == 0)
    def _():
        held[...] = jnp.zeros_like(held)

    for b, mask in enumerate(out_masks):
        block = jnp.concatenate([grad[pl.ds(start, part), :] for start in starts(mask)], axis=0)
        if b < stay:
            own_ref[b, 0] = block
        else:
            codes, level = code16(block)
            code_ref[b - stay, pl.ds(pl.multiple_of(head * rows, 16), rows), :] = codes
            held[b - stay, pl.ds(head, 1), :] = level

    @pl.when(head == chunk - 1)
    def _():
        last = code_ref.shape[1] - 16
        for b in range(stay):
            code_ref[b, last:, :] = pack_levels([held[b]])


def attention_call(head_width, masks, out_masks, place, bias_arrays, first, own_proj, sib_proj):
    blocks = len(masks)
    _, chunk, rows, tok = bias_arrays[0].shape
    count = own_proj[0].shape[0]
    stay = blocks // 2
    head = pl.BlockSpec((count, head_width, tok), lambda h, _: (0, first + h, 0))
    mixed = pl.BlockSpec((count, head_width, tok), lambda h, o: (0, h, 0))
    coded = (stay, chunk * rows + 16, tok)
    tiles = 2 * count * chunk
    return pl.pallas_call(
        functools.partial(attention_kernel, len(bias_arrays), head_width, masks, out_masks),
        grid_spec=pltpu.PrefetchScalarGridSpec(
            num_scalar_prefetch=1,
            grid=(chunk,),
            in_specs=[
                pl.BlockSpec((array.shape[0], 1, rows, tok), lambda h, o: (0, h, 0, 0)) for array in bias_arrays
            ]
            + [head] * 8,
            out_specs=[
                mixed,
                mixed,
                pl.BlockSpec((stay, 1, rows, tok), lambda h, o: (0, h, 0, 0)),
                pl.BlockSpec(coded, lambda h, o: (0, 0, 0)),
            ],
            scratch_shapes=[
                pltpu.VMEM((tok, tok), F32),
                pltpu.VMEM((tok, tok), F32),
                pltpu.VMEM((stay, 8, tok), F32),
            ],
        ),
        out_shape=[
            jax.ShapeDtypeStruct((count, chunk * head_width, tok), BF16),
            jax.ShapeDtypeStruct((count, chunk * head_width, tok), BF16),
            jax.ShapeDtypeStruct((stay, chunk, rows, tok), F32),
            jax.ShapeDtypeStruct(coded, jnp.int16),
        ],
        compiler_params=pltpu.CompilerParams(vmem_limit_bytes=VMEM_WIDE),
        cost_estimate=COST,
        name="attention",
    )(place, *bias_arrays, *own_proj, *sib_proj)


def plain_call(kernel, name, out_shape, *operands):
    vm = pl.BlockSpec(memory_space=pltpu.VMEM)
    return pl.pallas_call(
        kernel,
        in_specs=[vm] * len(operands),
        out_specs=[vm] * len(out_shape),
        out_shape=out_shape,
        compiler_params=pltpu.CompilerParams(vmem_limit_bytes=VMEM_LIMIT),
        cost_estimate=COST,
        name=name,
    )(*operands)


def concat_kernel(*refs):
    out_ref, at = refs[-1], 0
    for ref in refs[:-1]:
        out_ref[at : at + ref.shape[0]] = ref[...]
        at += ref.shape[0]


def concat_call(*arrays):
    blocks = sum(x.shape[0] for x in arrays)
    return plain_call(concat_kernel, "concat", [jax.ShapeDtypeStruct((blocks, *arrays[0].shape[1:]), BF16)], *arrays)[0]


def join_kernel(own_ref, code_ref, stay_ref, next_ref):
    blocks, chunk, rows, _ = own_ref.shape
    last = chunk * rows
    stay = blocks // 2
    for b in range(blocks):
        levels = code_ref[b, last:, :].astype(jnp.int32).astype(F32)
        held = []
        for h in range(chunk):
            span = slice(h * rows, (h + 1) * rows)
            block = own_ref[b, h] + decode16(code_ref[b, span, :], levels[h : h + 1])
            if b < stay:
                stay_ref[b, h] = block
            else:
                codes, level = code16(block)
                next_ref[b - stay, span, :] = codes
                held.append(level)
        if held:
            next_ref[b - stay, last:, :] = pack_levels(held)


def join_call(own, codes):
    blocks, chunk, rows, tok = own.shape
    return plain_call(
        join_kernel,
        "join",
        [
            jax.ShapeDtypeStruct((blocks // 2, chunk, rows, tok), F32),
            jax.ShapeDtypeStruct((blocks // 2, chunk * rows + 16, tok), jnp.int16),
        ],
        own, codes,
    )


def total_kernel(own_ref, code_ref, here_ref, there_ref):
    _, chunk, rows, _ = own_ref.shape
    part = rows // 2
    levels = code_ref[0, chunk * rows :, :].astype(jnp.int32).astype(F32)
    for h in range(chunk):
        block = own_ref[0, h] + decode16(code_ref[0, h * rows : (h + 1) * rows, :], levels[h : h + 1])
        here_ref[h] = block[:part]
        there_ref[h] = block[part:]


def total_call(own, codes):
    _, chunk, rows, tok = own.shape
    return plain_call(
        total_kernel, "last_join", [jax.ShapeDtypeStruct((chunk, rows // 2, tok), F32)] * 2, own, codes
    )


def output_kernel(parts, core_ref, *refs):
    own_refs, other_refs = refs[:parts], refs[parts : 2 * parts]
    w_own, w_other, mask_ref, out_ref = refs[2 * parts :]
    live = mask_ref[...] > 0
    total = None
    for group, weight in ((own_refs, w_own), (other_refs, w_other)):
        start = 0
        for ref in group:
            size = ref.shape[1]
            mixed = ref[0]
            mixed = jnp.where(live, mixed.astype(F32), 0.0).T.astype(BF16)
            term = dot(mixed, weight[start : start + size, :])
            total = term if total is None else total + term
            start += size
    out_ref[0] = total.astype(BF16)


def output_call(core, own, other, w_out, mask_row):
    samples, _, tok = own[0].shape
    parts = len(own)
    width = w_out.shape[0]
    half = width // 2
    blocks = [pl.BlockSpec((1, x.shape[1], tok), lambda s, c: (s, 0, 0)) for x in (*own, *other)]
    return pl.pallas_call(
        functools.partial(output_kernel, parts),
        grid_spec=pltpu.PrefetchScalarGridSpec(
            num_scalar_prefetch=1,
            grid=(samples,),
            in_specs=blocks
            + [
                pl.BlockSpec((half, width), lambda s, c: (c[0], 0)),
                pl.BlockSpec((half, width), lambda s, c: (1 - c[0], 0)),
                pl.BlockSpec((1, tok), lambda s, c: (0, 0)),
            ],
            out_specs=pl.BlockSpec((1, tok, width), lambda s, c: (s, 0, 0)),
        ),
        out_shape=jax.ShapeDtypeStruct((samples, tok, width), BF16),
        compiler_params=pltpu.CompilerParams(vmem_limit_bytes=VMEM_WIDE),
        cost_estimate=COST,
        name="output",
    )(core, *own, *other, w_out, w_out, mask_row)


def load_rows(refs, i):
    return jnp.concatenate([ref[:, i, :] for ref in refs], axis=0)


def projection_kernel(parts, core_ref, *refs):
    own_refs, other_refs = refs[:parts], refs[parts : 2 * parts]
    pair_ref, gain_ref, mean_ref, rstd_ref, out_ref = refs[2 * parts :]
    rows, tok, chan = pair_ref.shape
    heads = out_ref.shape[0]
    half = heads // 2
    total = jnp.zeros((3 * heads, chan), F32)
    means = jnp.zeros((heads, tok), F32)
    for i in range(rows):
        grads = load_rows([*own_refs, *other_refs], i) * rstd_ref[i : i + 1, :]
        means = means + grads * mean_ref[i : i + 1, :]
        total = total + dot(jnp.concatenate(pieces3(grads), axis=0), pair_ref[i])
    raw = total[:heads] + (total[heads : 2 * heads] + total[2 * heads :])
    result = (raw - jnp.sum(means, axis=1, keepdims=True)) * gain_ref[...]
    core = core_ref[0]
    out_ref[pl.ds(pl.multiple_of(core * half, half), half), :] = result[:half]
    out_ref[pl.ds(pl.multiple_of((1 - core) * half, half), half), :] = result[half:]


def pair_grad_kernel(parts, core_ref, *refs):
    own_refs, other_refs = refs[:parts], refs[parts : 2 * parts]
    pair_ref, gain_ref, wt_ref, mean_ref, rstd_ref, bias_ref, out_ref, turned = refs[2 * parts :]
    rows, tok, chan = pair_ref.shape
    half = wt_ref.shape[1] // 2
    core = core_ref[0]
    turned[...] = wt_ref[...].astype(F32).T

    def own_first(take):
        return jnp.concatenate([take(core * half), take((1 - core) * half)], axis=0)

    scaled = own_first(lambda at: turned[pl.ds(pl.multiple_of(at, half), half), :]) * gain_ref[...]
    scaled = scaled - jnp.mean(scaled, axis=1, keepdims=True)
    wh, wm, wl = pieces3(scaled)
    project = jnp.concatenate([wh, wm, wh, wl, wm, wh], axis=0)
    count = project.shape[0]
    zero, one = jnp.zeros((8, chan), BF16), jnp.ones((8, chan), BF16)
    right = jnp.concatenate(
        [
            jnp.concatenate([project, jnp.zeros_like(project)], axis=1),
            jnp.concatenate([one, zero], axis=1),
            jnp.concatenate([zero, one], axis=1),
        ],
        axis=0,
    )
    fill = jnp.zeros((5, tok), F32)
    for i in range(rows):
        rstd = rstd_ref[i : i + 1, :]
        grads = load_rows([*own_refs, *other_refs], i) * rstd
        bias = own_first(lambda at: bias_ref[pl.ds(at, half), i, :])
        along = jnp.sum(grads * bias, axis=0, keepdims=True) * rstd * (1.0 / chan)
        gh, gm, gl = pieces3(grads)
        back = [piece.astype(F32) for piece in pieces3(along * mean_ref[i : i + 1, :])]
        slope = [piece.astype(F32) for piece in pieces3(along)]
        extra = jnp.concatenate([*back, fill, *slope, fill], axis=0).astype(BF16)
        left = jnp.concatenate([gh, gh, gm, gh, gm, gl, extra], axis=0)
        both = dot(left, right, TN)
        out_ref[i] = (both[:, :chan] - pair_ref[i].astype(F32) * both[:, chan:]).astype(BF16)


def final_call(kernel, name, core, own, other, operands, out_shape, scratch=()):
    vm = pl.BlockSpec(memory_space=pltpu.VMEM)
    parts = len(own)
    return pl.pallas_call(
        functools.partial(kernel, parts),
        in_specs=[pl.BlockSpec(memory_space=pltpu.SMEM)] + [vm] * (2 * parts + len(operands)),
        out_specs=vm,
        out_shape=out_shape,
        scratch_shapes=scratch,
        compiler_params=pltpu.CompilerParams(vmem_limit_bytes=VMEM_LIMIT),
        cost_estimate=COST,
        name=name,
    )(core, *own, *other, *operands)


def per_device_tiled(
    chips, activations, cotangent, pair_rep, pair_gain, w_pair, w_query, w_key, w_value, w_out, token_mask
):
    rows, tok, chan = pair_rep.shape
    heads = w_pair.shape[1]
    half = heads // 2
    head_width = w_query.shape[0] // heads
    core = lax.axis_index("core")
    chip = lax.axis_index("chip")
    bits = [1 << b for b in reversed(range(chips.bit_length() - 1))]

    def swap_core(x):
        return lax.ppermute(x, "core", [(0, 1), (1, 0)])

    def swap(x, bit):
        return lax.ppermute(x, "chip", [(c, c ^ bit) for c in range(chips)])

    tie = lax.optimization_barrier
    place = jnp.stack([chip, core]).astype(jnp.int32)
    core_1 = core.reshape(1).astype(jnp.int32)
    gain = pair_gain.reshape(1, chan)
    normal, other = bits, [*bits[:-2], bits[-1], bits[-2]]
    count, levels = len(CHUNKS), len(bits)
    gather_bits = [other if n in GATHER_OTHER else normal for n in range(count)]
    scatter_bits = [list(reversed(other if n in SCATTER_OTHER else normal)) for n in range(count)]

    def masks_of(order):
        masks = [0]
        for bit in order:
            masks = masks + [m ^ bit for m in masks]
        return masks

    sib_act, sib_cot = swap_core(activations), swap_core(cotangent)
    bias_own, bias_other, mean_rows, rstd_rows, bias_rows = bias_call(core_1, pair_rep, gain, w_pair, token_mask)
    bias_chip = jnp.concatenate([bias_own, swap_core(bias_other)], axis=1)[None]
    mask_row = token_mask.reshape(1, tok)
    weights = (w_query, w_key, w_value, w_out)
    own_proj = project_call(core_1, activations, cotangent, *weights, mask_row)
    sib_proj = project_call(core_1, sib_act, sib_cot, *weights, mask_row)

    firsts = [sum(CHUNKS[:n]) for n in range(count)]
    arrays = []
    for n, size in enumerate(CHUNKS):
        mine = bias_chip[:, firsts[n] : firsts[n] + size]
        for level, bit in enumerate(gather_bits[n][:-1]):
            coming = swap(mine, bit)
            if n == 0 and level == 0:
                coming, own_proj = tie((coming, own_proj))
            if n == 0 and level == 1:
                coming, sib_proj = tie((coming, sib_proj))
            mine = concat_call(mine, coming)
        arrays.append([mine, swap(mine, gather_bits[n][-1])])

    mixed_own, mixed_other, grads_own, grads_other = [], [], [], []
    far = [None] * count
    stays = [None] * count
    level_of = [0] * count

    def join(n):
        level_of[n] += 1
        stays[n], codes = join_call(stays[n], far[n])
        return codes

    for n in range(count):
        if n == count - 1 and n >= EARLY:
            for k in range(n - EARLY + 1):
                codes = join(k)
                codes, place = tie((codes, place))
                far[k] = swap(codes, scatter_bits[k][1])
        mixed0, mixed1, stays[n], codes = attention_call(
            head_width, masks_of(gather_bits[n]), masks_of(reversed(scatter_bits[n])),
            place, arrays[n], firsts[n], own_proj, sib_proj,
        )
        mixed_own.append(mixed0)
        mixed_other.append(mixed1)
        far[n] = swap(codes, scatter_bits[n][0])
    if LATE:
        first_join = join(1)
        first_join, *mixed_other = tie((first_join, *mixed_other))
        far[1] = swap(first_join, scatter_bits[1][1])
    mixed_other = [swap_core(mixed1) for mixed1 in mixed_other]
    attended = output_call(core_1, mixed_own, mixed_other, w_out, mask_row)
    for n in range(count):
        while level_of[n] < levels - 1:
            codes = join(n)
            far[n] = swap(codes, scatter_bits[n][level_of[n]])
    far, attended = tie((far, attended))
    for n in range(count):
        here, there = total_call(stays[n], far[n])
        grads_own.append(here)
        grads_other.append(swap_core(there))

    projection = final_call(
        projection_kernel, "pair_projection", core_1, grads_own, grads_other,
        (pair_rep, gain, mean_rows, rstd_rows), jax.ShapeDtypeStruct((heads, chan), F32),
    )
    rstd_rows, projection = tie((rstd_rows, projection))
    grad_pair = final_call(
        pair_grad_kernel, "pair_gradient", core_1, grads_own, grads_other,
        (pair_rep, gain, w_pair, mean_rows, rstd_rows, bias_rows), jax.ShapeDtypeStruct(pair_rep.shape, BF16),
        (pltpu.VMEM((heads, chan), F32),),
    )
    projection = projection + swap_core(projection)
    for bit in reversed(bits):
        other = swap(projection, bit)
        if bit == bits[-1]:
            other, grad_pair = tie((other, grad_pair))
        projection = projection + other
    return (attended, grad_pair, projection.T)


def solution(mesh):
    split = P(("grp", "smp"), None, None)
    devices = mesh.shape["smp"]

    def run(activations, cotangent, pair_rep, pair_gain, w_pair, *rest):
        parts = mesh.shape["grp"]
        rows, heads, tok = pair_rep.shape[0] // (parts * devices), w_pair.shape[1], pair_rep.shape[1]
        power = devices >= 8 and devices & (devices - 1) == 0
        if power and rows % 8 == 0 and rows <= 128 and heads == 2 * sum(CHUNKS) and tok % 128 == 0:
            inner = Mesh(mesh.devices.reshape(parts, devices // 2, 2), ("grp", "chip", "core"))
            whole = P(("grp", "chip", "core"), None, None)
            body = functools.partial(per_device_tiled, devices // 2)
        else:
            inner, whole, body = mesh, split, per_device_plain
        return jax.shard_map(
            body,
            mesh=inner,
            in_specs=(whole, whole, whole, P(), P(), P(), P(), P(), P(), P("grp")),
            out_specs=(whole, whole, P("grp", None)),
            check_vma=False,
        )(activations, cotangent, pair_rep, pair_gain, w_pair, *rest)

    return run
```
